512 devices in a mesh: rep: 32 (over x, z_lo, core), fsdp: 16 (over z_hi, y).
Axes of the slice: x: 4, y: 8, z: 8 (z_hi: 2, z_lo: 4; z = z_hi * 4 + z_lo), core: 2. Of those that a mesh axis runs over, the one named last changes fastest.
Arguments:
- local_params: bfloat16 [32, 256, 45056], P('rep', None, 'fsdp'), may hold values from -40 to 40
- base_params: bfloat16 [256, 45056], P(None, 'fsdp'), may hold values from -3 to 3
- momentum: float32 [256, 45056], P('rep', 'fsdp'), may hold values from -3 to 3
- encode_exponents: int32 [2, 352], P(None, 'fsdp'), may hold values from -9 to -5
- return_exponents: int32 [2, 352], P(None, 'fsdp'), may hold values from -12 to -8
Outputs:
- new_params: bfloat16 [256, 45056], P(None, 'fsdp')
- new_momentum: float32 [256, 45056], P('rep', 'fsdp')
The draws below stay inside these ranges and needn't reach their ends.
All inputs are finite; a program needn't handle non-finite values.
Results may differ from the reference program's by a relative error of at most 0.0065.
Values may be sent and summed in bfloat16 or wider, within the bound.
A program may use at most 64 MiB of HBM per device.

```python
import jax
import jax.numpy as jnp
from jax import lax

BLOCK = 128
ROWS = 256
COLS = 45056
REPLICAS = 32
N_REP = 32


def shared_exponents(key):
    inner = jax.random.fold_in(key, 101)
    return jax.random.randint(inner, (ROWS // BLOCK, COLS // BLOCK), -9, -4).astype(jnp.int32)


def shared_base(key):
    inner = jax.random.fold_in(key, 102)
    return jnp.clip(0.5 * jax.random.normal(inner, (ROWS, COLS), jnp.float32), -3.0, 3.0)


def draw_encode_exponents(key, part):
    return shared_exponents(key)


def draw_base_params(key, part):
    return shared_base(key).astype(jnp.bfloat16)


def draw_local_params(key, part):
    exponents = shared_exponents(key)
    base_wide = shared_base(key)
    key = jax.random.fold_in(key, 7)
    key_noise, key_heavy = jax.random.split(key)
    factor = jnp.exp2(exponents.astype(jnp.float32))
    scale_in = jnp.repeat(jnp.repeat(factor, BLOCK, axis=0), BLOCK, axis=1)
    noise = jnp.clip(jax.random.normal(key_noise, (REPLICAS, ROWS, COLS), jnp.float32), -6.0, 6.0)
    heavy = jax.random.bernoulli(key_heavy, 0.125, (REPLICAS, ROWS // BLOCK, COLS // BLOCK))
    boost = jnp.where(heavy, 4.0, 1.0).astype(jnp.float32)
    boost = jnp.repeat(jnp.repeat(boost, BLOCK, axis=1), BLOCK, axis=2)
    return (base_wide[None] + 40.0 * noise * boost * scale_in[None]).astype(jnp.bfloat16)


def plant(values, rng, smallest, high):
    place = [jax.random.randint(jax.random.fold_in(rng, axis), (), 0, length) for axis, length in enumerate(values.shape)]
    longest = values.shape.index(max(values.shape))
    neighbour = place[:longest] + [(place[longest] + 1) % values.shape[longest]] + place[longest + 1:]
    return values.at[tuple(place)].set(smallest).at[tuple(neighbour)].set(high)


def level_of(key, shape, pieces, least, high):
    def one(dim, parts):
        steps = jax.random.uniform(jax.random.fold_in(jax.random.fold_in(key, 6), dim), (parts,), jnp.float32, least / len(pieces), high / len(pieces))
        return jnp.repeat(jnp.exp(steps), shape[dim] // parts).reshape((-1,) + (1,) * (len(shape) - dim - 1))

    gain = one(*pieces[0])
    for cut in pieces[1:]:
        gain = gain * one(*cut)
    return gain


def normal_values(key, dims, width, most, cuts=(), dtype=jnp.bfloat16):
    drawn = width * jax.random.normal(key, dims, jnp.float32)
    if cuts:
        drawn = drawn * level_of(key, dims, cuts, -0.22, 0.18)
    return jnp.clip(drawn, -most, most).astype(dtype)


def setup_inputs(seed: int = 0) -> dict:
    arg_keys = jax.random.split(jax.random.key(seed), 6)
    return {
        "local_params": draw_local_params(jax.random.fold_in(arg_keys[5], 71), 0),
        "base_params": draw_base_params(jax.random.fold_in(arg_keys[5], 71), 0),
        "momentum": normal_values(arg_keys[2], (ROWS, COLS), 0.5, 3.0, ((0, 32), (1, 16)), jnp.float32),
        "encode_exponents": draw_encode_exponents(jax.random.fold_in(arg_keys[5], 71), 0),
        "return_exponents": plant(jax.random.randint(arg_keys[4], (ROWS // BLOCK, COLS // BLOCK), -12, -7), jax.random.fold_in(arg_keys[4], 1), -12, (-7) - 1).astype(jnp.int32),
    }


CODE_LIMIT = 448.0
MOMENTUM_RATE = 0.9
OUTER_RATE = 0.7


def expand(exponents):
    factor = jnp.exp2(exponents.astype(jnp.float32))
    return jnp.repeat(jnp.repeat(factor, BLOCK, axis=0), BLOCK, axis=1)


def reference(local_params, base_params, momentum, encode_exponents, return_exponents):
    scale_in = expand(encode_exponents)
    scale_out = expand(return_exponents)
    base_wide = base_params.astype(jnp.float32)

    def accumulate(summed, replica):
        encoded = jnp.clip((replica.astype(jnp.float32) - base_wide) / scale_in, -CODE_LIMIT, CODE_LIMIT).astype(jnp.bfloat16)
        return summed + encoded.astype(jnp.float32), None

    summed, _ = lax.scan(accumulate, jnp.zeros(base_wide.shape, jnp.float32), local_params)
    outer_grad = summed * scale_in / N_REP
    new_momentum = MOMENTUM_RATE * momentum + outer_grad
    outer_step = OUTER_RATE * (outer_grad + MOMENTUM_RATE * new_momentum)
    delta_code = jnp.clip(outer_step / scale_out, -CODE_LIMIT, CODE_LIMIT).astype(jnp.bfloat16)
    new_params = (base_wide + delta_code.astype(jnp.float32) * scale_out).astype(jnp.bfloat16)
    return new_params, new_momentum
```

```python
import functools

import jax
import jax.numpy as jnp
from jax import lax
from jax.experimental import pallas as pl
from jax.experimental.pallas import tpu as pltpu
from jax.sharding import PartitionSpec as P

BLOCK = 128
CODE_LIMIT = 448.0
MOMENTUM_RATE = 0.9
OUTER_RATE = 0.7
MESH = pl.DeviceIdType.MESH
NX, NZ = 4, 4
XROWS, ZROWS = 64, 16
HALF = XROWS // 2
CHUNKS = ((0, 4), (4, 8), (8, 11))
BF16, F32 = jnp.bfloat16, jnp.float32


def power_of_two(exponent):
    size = jnp.abs(exponent)
    result = jnp.ones(exponent.shape, F32)
    for bit in range(7):
        up, down = 2.0 ** (1 << bit) if bit < 7 else 1.0, 2.0 ** -(1 << bit)
        factor = jnp.where(exponent < 0, down, up)
        result = result * jnp.where((size & (1 << bit)) != 0, factor, 1.0)
    return result


def kernel(
    params, base, momentum, enc_exp, ret_exp, new_params, new_momentum,
    own_params, sib_params, own_base, oth_base, exps, enc_mul, enc_scale, ret_mul, ret_scale,
    s_far, s_right, s_left, f_up, f_dn, x_left, x_right, t_wide, t_narrow, z_in,
    moment, moment_out, moment_in, codes, sib_codes, own_out, oth_out,
    local_sem, send_sem, recv_sem,
):
    rep = lax.axis_index("rep")
    x, z, c = rep // (NZ * 2), (rep // 2) % NZ, rep % 2
    tiles = own_params.shape[1] // BLOCK
    width = tiles * BLOCK

    def place(px, pz, pc):
        return {"rep": (px * NZ + pz) * 2 + pc}

    sibling = place(x, z, 1 - c)
    right, left, far = (x + 1) % NX, (x + 3) % NX, (x + 2) % NX
    x_right_dev, x_left_dev = place(right, z, c), place(left, z, c)
    z_devs = [place(x, (z + d) % NZ, c) for d in (1, 2, 3)]

    def rows_of(block, first=0, count=XROWS):
        return pl.ds(pl.multiple_of(block * XROWS + first, 16), count)

    own_cols = pl.ds(pl.multiple_of(c * width, BLOCK), width)
    oth_cols = pl.ds(pl.multiple_of((1 - c) * width, BLOCK), width)

    counts = {"local": 0, "remote": 0}
    sends = []

    def local(src, dst):
        i = counts["local"]
        counts["local"] += 1
        copy = pltpu.make_async_copy(src, dst, local_sem.at[i])
        copy.start()
        return copy

    def remote(src, dst, device):
        i = counts["remote"]
        counts["remote"] += 1
        copy = pltpu.make_async_remote_copy(
            src_ref=src, dst_ref=dst, send_sem=send_sem.at[i], recv_sem=recv_sem.at[i],
            device_id=device, device_id_type=MESH,
        )
        copy.start()
        sends.append(copy)
        return copy

    order = (far, right, left, x)
    loads = []
    for block in order:
        rows = rows_of(block)
        loads.append((
            local(base.at[rows, own_cols], own_base.at[rows]),
            local(params.at[0, rows, own_cols], own_params.at[rows]),
        ))
    moment_rows = pl.ds(pl.multiple_of(c * 8, 8), 8)
    other_rows = pl.ds(pl.multiple_of((1 - c) * 8, 8), 8)
    moment_load = local(momentum.at[:, own_cols], moment.at[moment_rows])
    oth_base_load = local(base.at[:, oth_cols], oth_base)

    barrier = pltpu.get_barrier_semaphore()
    for device in [sibling, x_right_dev, x_left_dev] + z_devs:
        pl.semaphore_signal(barrier, inc=1, device_id=device, device_id_type=MESH)

    for half in range(2):
        for row in range(2):
            for tile in range(tiles):
                at = (half * 2 + row) * tiles + tile
                column = tile + (c if half == 0 else 1 - c) * tiles
                if half == 0:
                    exps[0, pl.ds(at, 1), :] = jnp.full((1, BLOCK), enc_exp[row, column], jnp.int32)
                exps[1, pl.ds(at, 1), :] = jnp.full((1, BLOCK), ret_exp[row, column], jnp.int32)
    encode_exps = exps[0, 0:2 * tiles, :]
    return_exps = exps[1, 0:4 * tiles, :]
    enc_mul[0:2 * tiles, :] = power_of_two(-encode_exps)
    enc_scale[0:2 * tiles, :] = power_of_two(encode_exps)
    ret_mul[0:4 * tiles, :] = power_of_two(-return_exps)
    ret_scale[0:4 * tiles, :] = power_of_two(return_exps)

    pl.semaphore_wait(barrier, 6)

    swaps = []
    for block in order:
        rows = rows_of(block)
        swaps.append(remote(params.at[0, rows, oth_cols], sib_params.at[rows], sibling))
    moment_swap = remote(momentum.at[:, oth_cols], moment.at[moment_rows], sibling)

    ready = set()

    def need(which):
        if which not in ready:
            ready.add(which)
            for copy in loads[which]:
                copy.wait()
            swaps[which].wait_recv()

    def encoded_pair(which, tile):
        block = order[which]
        rows = rows_of(block)
        lanes = slice(tile * BLOCK, (tile + 1) * BLOCK)
        factor = enc_mul[pl.ds((block // 2) * tiles + tile, 1), :]
        start = own_base[rows, lanes].astype(F32)
        total = None
        for source in (own_params, sib_params):
            code = jnp.clip((source[rows, lanes].astype(F32) - start) * factor, -CODE_LIMIT, CODE_LIMIT)
            code = code.astype(BF16).astype(F32)
            total = code if total is None else total + code
        return total

    state = [dict() for _ in CHUNKS]
    upper, lower = pl.ds(0, HALF), pl.ds(HALF, HALF)

    def far_stage(k):
        lo, hi = CHUNKS[k]
        need(0)
        for tile in range(lo, hi):
            s_far[tile] = encoded_pair(0, tile).astype(BF16)
        part = pl.ds(lo, hi - lo)
        state[k]["up"] = remote(s_far.at[part, upper], f_up.at[part], x_right_dev)
        state[k]["dn"] = remote(s_far.at[part, lower], f_dn.at[part], x_left_dev)

    def near_stage(k):
        lo, hi = CHUNKS[k]
        part = pl.ds(lo, hi - lo)
        need(1)
        for tile in range(lo, hi):
            s_right[tile] = encoded_pair(1, tile).astype(BF16)
        state[k]["raw_r"] = remote(s_right.at[part, lower], x_left.at[part, lower], x_right_dev)
        need(2)
        for tile in range(lo, hi):
            s_left[tile] = encoded_pair(2, tile).astype(BF16)
        state[k]["raw_l"] = remote(s_left.at[part, upper], x_right.at[part, upper], x_left_dev)

    def join_stage(k):
        lo, hi = CHUNKS[k]
        part = pl.ds(lo, hi - lo)
        state[k]["up"].wait_recv()
        for tile in range(lo, hi):
            s_right[tile, 0:HALF] = (s_right[tile, 0:HALF].astype(F32) + f_up[tile].astype(F32)).astype(BF16)
        state[k]["sum_r"] = remote(s_right.at[part, upper], x_left.at[part, upper], x_right_dev)
        state[k]["dn"].wait_recv()
        for tile in range(lo, hi):
            s_left[tile, HALF:XROWS] = (s_left[tile, HALF:XROWS].astype(F32) + f_dn[tile].astype(F32)).astype(BF16)
        state[k]["sum_l"] = remote(s_left.at[part, lower], x_right.at[part, lower], x_left_dev)

    def line_stage(k):
        lo, hi = CHUNKS[k]
        part = pl.ds(lo, hi - lo)
        need(3)
        for name in ("raw_r", "raw_l", "sum_r", "sum_l"):
            state[k][name].wait_recv()
        for tile in range(lo, hi):
            total = encoded_pair(3, tile) + x_left[tile].astype(F32) + x_right[tile].astype(F32)
            t_wide[tile] = total
            t_narrow[tile] = total.astype(BF16)
        state[k]["z"] = []
        for d in (2, 1, 3):
            rows = pl.ds(pl.multiple_of(((z + d) % NZ) * ZROWS, ZROWS), ZROWS)
            state[k]["z"].append(remote(t_narrow.at[part, rows], z_in.at[d - 1, part], z_devs[d - 1]))

    own_rows = pl.ds(pl.multiple_of(z * ZROWS, ZROWS), ZROWS)
    code_rows = pl.ds(pl.multiple_of(x * XROWS + z * ZROWS, ZROWS), ZROWS)

    def step_stage(k):
        lo, hi = CHUNKS[k]
        part = pl.ds(lo, hi - lo)
        if k == 0:
            moment_load.wait()
            moment_swap.wait_recv()
        for copy in state[k]["z"]:
            copy.wait_recv()
        for tile in range(lo, hi):
            lanes = slice(tile * BLOCK, (tile + 1) * BLOCK)
            at = pl.ds((x // 2) * tiles + tile, 1)
            summed = t_wide[tile, own_rows]
            for d in range(3):
                summed = summed + z_in[d, tile].astype(F32)
            outer_grad = summed * (enc_scale[at, :] * (1.0 / 32.0))
            new_moment = MOMENTUM_RATE * moment[:, lanes] + outer_grad
            moment_out[:, lanes] = new_moment
            outer_step = OUTER_RATE * (outer_grad + MOMENTUM_RATE * new_moment)
            code = jnp.clip(outer_step * ret_mul[at, :], -CODE_LIMIT, CODE_LIMIT)
            codes[tile, code_rows] = code.astype(BF16)
        state[k]["zg"] = [
            remote(codes.at[part, code_rows], codes.at[part, code_rows], z_devs[d - 1]) for d in (2, 1, 3)
        ]

    def ring_stage(k):
        lo, hi = CHUNKS[k]
        part = pl.ds(lo, hi - lo)
        for copy in state[k]["zg"]:
            copy.wait_recv()
        up, dn = rows_of(x, 0, HALF), rows_of(x, HALF, HALF)
        st = state[k]
        st["g_ru"] = remote(codes.at[part, up], codes.at[part, up], x_right_dev)
        st["g_ld"] = remote(codes.at[part, dn], codes.at[part, dn], x_left_dev)
        st["g_rd"] = remote(codes.at[part, dn], codes.at[part, dn], x_right_dev)
        st["g_lu"] = remote(codes.at[part, up], codes.at[part, up], x_left_dev)
        rows = rows_of(x)
        st["c"] = [remote(codes.at[part, rows], sib_codes.at[part, rows], sibling)]

    def pass_stage(k):
        lo, hi = CHUNKS[k]
        part = pl.ds(lo, hi - lo)
        st = state[k]
        st["g_ru"].wait_recv()
        rows = rows_of(left, 0, HALF)
        st["p_r"] = remote(codes.at[part, rows], codes.at[part, rows], x_right_dev)
        st["g_ld"].wait_recv()
        rows = rows_of(right, HALF, HALF)
        st["p_l"] = remote(codes.at[part, rows], codes.at[part, rows], x_left_dev)
        st["g_rd"].wait_recv()
        rows = rows_of(left)
        st["c"].append(remote(codes.at[part, rows], sib_codes.at[part, rows], sibling))
        st["g_lu"].wait_recv()
        rows = rows_of(right)
        st["c"].append(remote(codes.at[part, rows], sib_codes.at[part, rows], sibling))

    def last_stage(k):
        lo, hi = CHUNKS[k]
        part = pl.ds(lo, hi - lo)
        st = state[k]
        st["p_r"].wait_recv()
        st["p_l"].wait_recv()
        rows = rows_of(far)
        st["c"].append(remote(codes.at[part, rows], sib_codes.at[part, rows], sibling))

    stores = []
    first_other = []

    def apply(k, block, own):
        lo, hi = CHUNKS[k]
        rows = rows_of(block)
        if not own and not first_other:
            first_other.append(True)
            oth_base_load.wait()
        source, start, out = (codes, own_base, own_out) if own else (sib_codes, oth_base, oth_out)
        for tile in range(lo, hi):
            lanes = slice(tile * BLOCK, (tile + 1) * BLOCK)
            at = pl.ds(((0 if own else 2) + block // 2) * tiles + tile, 1)
            update = source[tile, rows].astype(F32) * ret_scale[at, :]
            out[rows, lanes] = (start[rows, lanes].astype(F32) + update).astype(BF16)
        columns = pl.ds(
            pl.multiple_of((c if own else 1 - c) * width + lo * BLOCK, BLOCK), (hi - lo) * BLOCK
        )
        stores.append(local(
            out.at[rows, pl.ds(lo * BLOCK, (hi - lo) * BLOCK)], new_params.at[rows, columns]
        ))

    def apply_other(k, i):
        state[k]["c"][i].wait_recv()
        apply(k, (x, left, right, far)[i], False)

    far_stage(0)
    far_stage(1)
    far_stage(2)
    near_stage(0)
    near_stage(1)
    join_stage(0)
    near_stage(2)
    join_stage(1)
    line_stage(0)
    join_stage(2)
    line_stage(1)
    step_stage(0)
    line_stage(2)
    step_stage(1)
    ring_stage(0)
    step_stage(2)
    ring_stage(1)
    back = remote(moment_out.at[other_rows], moment_in, sibling)
    stores.append(local(moment_out.at[moment_rows], new_momentum.at[:, own_cols]))
    pass_stage(0)
    ring_stage(2)
    apply(0, x, True)
    apply(1, x, True)
    apply(0, left, True)
    apply(0, right, True)
    pass_stage(1)
    last_stage(0)
    back.wait_recv()
    stores.append(local(moment_in, new_momentum.at[:, oth_cols]))
    apply(2, x, True)
    apply_other(0, 0)
    apply_other(1, 0)
    apply_other(2, 0)
    apply_other(0, 1)
    apply_other(0, 2)
    pass_stage(2)
    last_stage(1)
    apply(0, far, True)
    apply_other(0, 3)
    apply(1, left, True)
    apply(1, right, True)
    apply_other(1, 1)
    apply_other(1, 2)
    apply(2, left, True)
    apply(2, right, True)
    apply(1, far, True)
    apply_other(1, 3)
    last_stage(2)
    apply_other(2, 1)
    apply_other(2, 2)
    apply(2, far, True)
    apply_other(2, 3)

    for copy in sends:
        copy.wait_send()
    for copy in stores:
        copy.wait()


def on_device(local_params, base_params, momentum, encode_exponents, return_exponents):
    _, rows, columns = local_params.shape
    width = columns // 2
    tiles = width // BLOCK
    table = pltpu.VMEM((-(-4 * tiles // 8) * 8, BLOCK), F32)
    half = pltpu.VMEM((rows, width), BF16)
    block = pltpu.VMEM((tiles, XROWS, BLOCK), BF16)
    half_block = pltpu.VMEM((tiles, HALF, BLOCK), BF16)
    any_space = pl.BlockSpec(memory_space=pltpu.HBM)
    scalars = pl.BlockSpec(memory_space=pltpu.SMEM)
    return pl.pallas_call(
        kernel,
        name="outer_step",
        out_shape=(
            jax.ShapeDtypeStruct((rows, columns), BF16),
            jax.ShapeDtypeStruct(momentum.shape, F32),
        ),
        in_specs=[any_space, any_space, any_space, scalars, scalars],
        out_specs=(any_space, any_space),
        scratch_shapes=[
            half, half, half, half,
            pltpu.VMEM((2, -(-4 * tiles // 8) * 8, BLOCK), jnp.int32),
            table, table, table, table,
            block, block, block, half_block, half_block, block, block,
            pltpu.VMEM((tiles, XROWS, BLOCK), F32),
            block,
            pltpu.VMEM((3, tiles, ZROWS, BLOCK), BF16),
            pltpu.VMEM((ZROWS, width), F32),
            pltpu.VMEM((ZROWS, width), F32),
            pltpu.VMEM((8, width), F32),
            pltpu.VMEM((tiles, rows, BLOCK), BF16),
            pltpu.VMEM((tiles, rows, BLOCK), BF16),
            half, half,
            pltpu.SemaphoreType.DMA((48,)),
            pltpu.SemaphoreType.DMA((96,)),
            pltpu.SemaphoreType.DMA((96,)),
        ],
        compiler_params=pltpu.CompilerParams(
            collective_id=0, has_side_effects=True, vmem_limit_bytes=32 * 2**20
        ),
        cost_estimate=pl.CostEstimate(flops=20_000_000, bytes_accessed=4_500_000, transcendentals=0),
    )(local_params, base_params, momentum, encode_exponents, return_exponents)


def solution(mesh):
    return jax.shard_map(
        on_device,
        mesh=mesh,
        in_specs=(
            P("rep", None, "fsdp"),
            P(None, "fsdp"),
            P("rep", "fsdp"),
            P(None, "fsdp"),
            P(None, "fsdp"),
        ),
        out_specs=(P(None, "fsdp"), P("rep", "fsdp")),
        check_vma=False,
    )
```

```python
import jax
import jax.numpy as jnp
from jax import lax
from jax.experimental import pallas as pl
from jax.experimental.pallas import tpu as pltpu
from jax.sharding import PartitionSpec as P

BLOCK = 128
CODE_LIMIT = 448.0
MOMENTUM_RATE = 0.9
OUTER_RATE = 0.7
MESH = pl.DeviceIdType.MESH
NX, NZ = 4, 4
XROWS, ZROWS = 64, 16
HALF = XROWS // 2
CHUNKS = ((0, 4), (4, 8), (8, 11))
BF16, F32 = jnp.bfloat16, jnp.float32
LOADS = ("block0", "block1", "block2", "block3", "exponents", "other_base", "params_out", "moment_out")
SENDS = ("swap", "moment", "far", "right", "left", "line", "codes", "ring", "pass", "core", "moment_back")
ARRIVALS = ("swap0", "swap1", "swap2", "swap3", "moment", "moment_back") + tuple(
    f"{name}{k}"
    for k in range(len(CHUNKS))
    for name in ("up", "dn", "x", "line", "codes", "ring_r", "ring_l", "ring_n", "pass", "core_own", "core_near", "core_far")
)
SCHEDULE = (
    ("far", 0),
    ("far", 1),
    ("far", 2),
    ("near", 0),
    ("near", 1),
    ("join", 0),
    ("near", 2),
    ("join", 1),
    ("line", 0),
    ("join", 2),
    ("line", 1),
    ("step", 0),
    ("line", 2),
    ("step", 1),
    ("ring", 0),
    ("step", 2),
    ("ring", 1),
    ("moment_out",),
    ("pass", 0),
    ("ring", 2),
    ("own", 0, 0),
    ("own", 1, 0),
    ("own", 0, 1),
    ("own", 0, 2),
    ("pass", 1),
    ("last", 0),
    ("moment_in",),
    ("own", 2, 0),
    ("other", 0, 0),
    ("other", 1, 0),
    ("other", 2, 0),
    ("other", 0, 1),
    ("other", 0, 2),
    ("pass", 2),
    ("last", 1),
    ("own", 0, 3),
    ("other", 0, 3),
    ("own", 1, 1),
    ("own", 1, 2),
    ("other", 1, 1),
    ("other", 1, 2),
    ("own", 2, 1),
    ("own", 2, 2),
    ("own", 1, 3),
    ("other", 1, 3),
    ("last", 2),
    ("other", 2, 1),
    ("other", 2, 2),
    ("own", 2, 3),
    ("other", 2, 3),
)


def power_of_two(exponent):
    size = jnp.abs(exponent)
    result = jnp.ones(exponent.shape, F32)
    for bit in range(7):
        up, down = 2.0 ** (1 << bit), 2.0 ** -(1 << bit)
        factor = jnp.where(exponent < 0, down, up)
        result = result * jnp.where((size & (1 << bit)) != 0, factor, 1.0)
    return result


def kernel(
    params, base, momentum, enc_exp, ret_exp, new_params, new_momentum,
    exp_words, mine, sib_params, oth_base, exps, enc_mul, enc_scale, ret_mul, ret_scale,
    s_far, s_right, s_left, f_up, f_dn, x_in, t_wide, t_narrow, z_in,
    moment, moment_out, moment_in, codes, sib_codes, own_out, oth_out,
    load_sem, send_sem, recv_sem,
):
    rep = lax.axis_index("rep")
    x, z, c = rep // (NZ * 2), (rep // 2) % NZ, rep % 2
    width = sib_params.shape[1]
    tiles = width // BLOCK

    def place(px, pz, pc):
        return {"rep": (px * NZ + pz) * 2 + pc}

    sibling = place(x, z, 1 - c)
    right, left, far = (x + 1) % NX, (x + 3) % NX, (x + 2) % NX
    x_right_dev, x_left_dev = place(right, z, c), place(left, z, c)
    z_devs = [place(x, (z + d) % NZ, c) for d in (1, 2, 3)]

    def rows_of(block, first=0, count=XROWS):
        return pl.ds(pl.multiple_of(block * XROWS + first, 16), count)

    own_cols = pl.ds(pl.multiple_of(c * width, BLOCK), width)
    oth_cols = pl.ds(pl.multiple_of((1 - c) * width, BLOCK), width)

    def local(src, dst, name):
        pltpu.make_async_copy(src, dst, load_sem.at[LOADS.index(name)]).start()

    def remote(src, dst, device, send, arrival):
        pltpu.make_async_remote_copy(
            src_ref=src, dst_ref=dst, send_sem=send_sem.at[SENDS.index(send)],
            recv_sem=recv_sem.at[ARRIVALS.index(arrival)], device_id=device, device_id_type=MESH,
        ).start()

    def take(sem, ref):
        pltpu.make_async_copy(ref, ref, sem).wait()

    def loaded(name, ref):
        take(load_sem.at[LOADS.index(name)], ref)

    def arrived(name, ref):
        take(recv_sem.at[ARRIVALS.index(name)], ref)

    def sent(name, ref):
        take(send_sem.at[SENDS.index(name)], ref)

    local(enc_exp, exp_words.at[0], "exponents")
    local(ret_exp, exp_words.at[1], "exponents")
    order = (far, right, left, x)
    for which, block in enumerate(order):
        rows = rows_of(block)
        local(base.at[rows, own_cols], mine.at[0, rows], f"block{which}")
        local(params.at[0, rows, own_cols], mine.at[1, rows], f"block{which}")

    barrier = pltpu.get_barrier_semaphore()
    for device in [x_right_dev, x_left_dev] + z_devs + [sibling]:
        pl.semaphore_signal(barrier, inc=1, device_id=device, device_id_type=MESH)

    loaded("exponents", exp_words)
    for half in range(2):
        for row in range(2):
            for tile in range(tiles):
                at = (half * 2 + row) * tiles + tile
                column = tile + (c if half == 0 else 1 - c) * tiles
                if half == 0:
                    exps[0, pl.ds(at, 1), :] = jnp.full((1, BLOCK), exp_words[0, row, column], jnp.int32)
                exps[1, pl.ds(at, 1), :] = jnp.full((1, BLOCK), exp_words[1, row, column], jnp.int32)
    encode_exps = exps[0, 0:2 * tiles, :]
    return_exps = exps[1, 0:4 * tiles, :]
    enc_mul[0:2 * tiles, :] = power_of_two(-encode_exps)
    enc_scale[0:2 * tiles, :] = power_of_two(encode_exps)
    ret_mul[0:4 * tiles, :] = power_of_two(-return_exps)
    ret_scale[0:4 * tiles, :] = power_of_two(return_exps)

    pl.semaphore_wait(barrier, 6)

    for which, block in enumerate(order):
        rows = rows_of(block)
        remote(params.at[0, rows, oth_cols], sib_params.at[rows], sibling, "swap", f"swap{which}")
    moment_rows = pl.ds(pl.multiple_of(c * 8, 8), 8)
    other_rows = pl.ds(pl.multiple_of((1 - c) * 8, 8), 8)
    remote(momentum.at[:, oth_cols], moment.at[moment_rows], sibling, "moment", "moment")
    moment_load = pltpu.make_async_copy(
        momentum.at[:, own_cols], moment.at[moment_rows], recv_sem.at[ARRIVALS.index("moment")]
    )
    moment_load.start()
    local(base.at[:, oth_cols], oth_base, "other_base")

    ready = set()

    def need(which):
        if which not in ready:
            ready.add(which)
            rows = rows_of(order[which])
            loaded(f"block{which}", mine.at[:, rows])
            arrived(f"swap{which}", sib_params.at[rows])

    def encoded_pair(which, tile):
        block = order[which]
        rows = rows_of(block)
        lanes = slice(tile * BLOCK, (tile + 1) * BLOCK)
        factor = enc_mul[pl.ds((block // 2) * tiles + tile, 1), :]
        start = mine[0, rows, lanes].astype(F32)
        total = None
        for source in (mine[1, rows, lanes], sib_params[rows, lanes]):
            code = jnp.clip((source.astype(F32) - start) * factor, -CODE_LIMIT, CODE_LIMIT)
            code = code.astype(BF16).astype(F32)
            total = code if total is None else total + code
        return total

    upper, lower = pl.ds(0, HALF), pl.ds(HALF, HALF)

    def part_of(k):
        lo, hi = CHUNKS[k]
        return range(lo, hi), pl.ds(lo, hi - lo)

    def far_stage(k):
        need(0)
        span, part = part_of(k)
        for tile in span:
            s_far[tile] = encoded_pair(0, tile).astype(BF16)
        remote(s_far.at[part, upper], f_up.at[part], x_right_dev, "far", f"up{k}")
        remote(s_far.at[part, lower], f_dn.at[part], x_left_dev, "far", f"dn{k}")

    def near_stage(k):
        span, part = part_of(k)
        need(1)
        for tile in span:
            s_right[tile] = encoded_pair(1, tile).astype(BF16)
        remote(s_right.at[part, lower], x_in.at[0, part, lower], x_right_dev, "right", f"x{k}")
        need(2)
        for tile in span:
            s_left[tile] = encoded_pair(2, tile).astype(BF16)
        remote(s_left.at[part, upper], x_in.at[1, part, upper], x_left_dev, "left", f"x{k}")

    def join_stage(k):
        span, part = part_of(k)
        arrived(f"up{k}", f_up.at[part])
        for tile in span:
            s_right[tile, 0:HALF] = (s_right[tile, 0:HALF].astype(F32) + f_up[tile].astype(F32)).astype(BF16)
        remote(s_right.at[part, upper], x_in.at[0, part, upper], x_right_dev, "right", f"x{k}")
        arrived(f"dn{k}", f_dn.at[part])
        for tile in span:
            s_left[tile, HALF:XROWS] = (s_left[tile, HALF:XROWS].astype(F32) + f_dn[tile].astype(F32)).astype(BF16)
        remote(s_left.at[part, lower], x_in.at[1, part, lower], x_left_dev, "left", f"x{k}")

    def line_stage(k):
        span, part = part_of(k)
        need(3)
        arrived(f"x{k}", x_in.at[:, part])
        for tile in span:
            total = encoded_pair(3, tile) + x_in[0, tile].astype(F32) + x_in[1, tile].astype(F32)
            t_wide[tile] = total
            t_narrow[tile] = total.astype(BF16)
        for d in (2, 1, 3):
            rows = pl.ds(pl.multiple_of(((z + d) % NZ) * ZROWS, ZROWS), ZROWS)
            remote(t_narrow.at[part, rows], z_in.at[d - 1, part], z_devs[d - 1], "line", f"line{k}")

    own_rows = pl.ds(pl.multiple_of(z * ZROWS, ZROWS), ZROWS)
    code_rows = pl.ds(pl.multiple_of(x * XROWS + z * ZROWS, ZROWS), ZROWS)

    def step_stage(k):
        span, part = part_of(k)
        if k == 0:
            arrived("moment", moment)
        arrived(f"line{k}", z_in.at[:, part])
        for tile in span:
            lanes = slice(tile * BLOCK, (tile + 1) * BLOCK)
            at = pl.ds((x // 2) * tiles + tile, 1)
            summed = t_wide[tile, own_rows]
            for d in range(3):
                summed = summed + z_in[d, tile].astype(F32)
            outer_grad = summed * (enc_scale[at, :] * (1.0 / 32.0))
            new_moment = MOMENTUM_RATE * moment[:, lanes] + outer_grad
            moment_out[:, lanes] = new_moment
            outer_step = OUTER_RATE * (outer_grad + MOMENTUM_RATE * new_moment)
            code = jnp.clip(outer_step * ret_mul[at, :], -CODE_LIMIT, CODE_LIMIT)
            codes[tile, code_rows] = code.astype(BF16)
        mine_now = codes.at[part, code_rows]
        for d in (2, 1, 3):
            remote(mine_now, mine_now, z_devs[d - 1], "codes", f"codes{k}")

    def gathered(k, block, first=0, count=XROWS):
        return codes.at[part_of(k)[1], rows_of(block, first, count)]

    def to_sibling(k, block, arrival):
        part, rows = part_of(k)[1], rows_of(block)
        remote(codes.at[part, rows], sib_codes.at[part, rows], sibling, "core", arrival)

    def ring_stage(k):
        arrived(f"codes{k}", z_in.at[:, part_of(k)[1]])
        up, dn = gathered(k, x, 0, HALF), gathered(k, x, HALF, HALF)
        remote(up, up, x_right_dev, "ring", f"ring_r{k}")
        remote(dn, dn, x_left_dev, "ring", f"ring_l{k}")
        remote(dn, dn, x_right_dev, "ring", f"ring_n{k}")
        remote(up, up, x_left_dev, "ring", f"ring_n{k}")
        to_sibling(k, x, f"core_own{k}")

    def pass_stage(k):
        up, dn = gathered(k, left, 0, HALF), gathered(k, right, HALF, HALF)
        arrived(f"ring_r{k}", up)
        remote(up, up, x_right_dev, "pass", f"pass{k}")
        arrived(f"ring_l{k}", dn)
        remote(dn, dn, x_left_dev, "pass", f"pass{k}")
        arrived(f"ring_n{k}", gathered(k, x))
        to_sibling(k, left, f"core_near{k}")
        to_sibling(k, right, f"core_near{k}")

    def last_stage(k):
        arrived(f"pass{k}", gathered(k, far))
        to_sibling(k, far, f"core_far{k}")

    def apply(k, block, own):
        span, part = part_of(k)
        rows = rows_of(block)
        if not own and "other_base" not in ready:
            ready.add("other_base")
            loaded("other_base", oth_base)
        out = own_out if own else oth_out
        for tile in span:
            lanes = slice(tile * BLOCK, (tile + 1) * BLOCK)
            at = pl.ds(((0 if own else 2) + block // 2) * tiles + tile, 1)
            code = (codes if own else sib_codes)[tile, rows].astype(F32)
            start = mine[0, rows, lanes] if own else oth_base[rows, lanes]
            out[rows, lanes] = (start.astype(F32) + code * ret_scale[at, :]).astype(BF16)
        first, count = span.start * BLOCK, len(span) * BLOCK
        columns = pl.ds(pl.multiple_of((c if own else 1 - c) * width + first, BLOCK), count)
        local(out.at[rows, pl.ds(first, count)], new_params.at[rows, columns], "params_out")

    def own_stage(k, i):
        apply(k, (x, left, right, far)[i], True)

    def other_stage(k, i):
        if i == 0:
            arrived(f"core_own{k}", gathered(k, x))
        elif i == 1:
            arrived(f"core_near{k}", codes.at[part_of(k)[1], pl.ds(0, 2 * XROWS)])
        elif i == 3:
            arrived(f"core_far{k}", gathered(k, x))
        apply(k, (x, left, right, far)[i], False)

    def send_moment():
        remote(moment_out.at[other_rows], moment_in, sibling, "moment_back", "moment_back")
        local(moment_out.at[moment_rows], new_momentum.at[:, own_cols], "moment_out")

    def take_moment():
        arrived("moment_back", moment_in)
        local(moment_in, new_momentum.at[:, oth_cols], "moment_out")

    stages = {
        "far": far_stage, "near": near_stage, "join": join_stage, "line": line_stage, "step": step_stage,
        "ring": ring_stage, "pass": pass_stage, "last": last_stage, "own": own_stage, "other": other_stage,
        "moment_out": send_moment, "moment_in": take_moment,
    }
    for name, *where in SCHEDULE:
        stages[name](*where)

    sent("swap", sib_params)
    sent("moment", moment_in)
    sent("far", s_far)
    sent("right", s_right)
    sent("left", s_left)
    sent("line", z_in)
    sent("codes", z_in)
    sent("ring", codes.at[:, pl.ds(0, 2 * XROWS)])
    sent("pass", codes.at[:, pl.ds(0, XROWS)])
    sent("core", codes)
    sent("moment_back", moment_in)
    loaded("params_out", new_params)
    loaded("moment_out", new_momentum)


def on_device(local_params, base_params, momentum, encode_exponents, return_exponents):
    _, rows, columns = local_params.shape
    width = columns // 2
    tiles = width // BLOCK
    table = pltpu.VMEM((-(-4 * tiles // 8) * 8, BLOCK), F32)
    half = pltpu.VMEM((rows, width), BF16)
    block = pltpu.VMEM((tiles, XROWS, BLOCK), BF16)
    half_block = pltpu.VMEM((tiles, HALF, BLOCK), BF16)
    any_space = pl.BlockSpec(memory_space=pltpu.HBM)
    return pl.pallas_call(
        kernel,
        name="outer_step",
        out_shape=(
            jax.ShapeDtypeStruct((rows, columns), BF16),
            jax.ShapeDtypeStruct(momentum.shape, F32),
        ),
        in_specs=[any_space] * 5,
        out_specs=(any_space, any_space),
        scratch_shapes=[
            pltpu.SMEM((2,) + encode_exponents.shape, jnp.int32),
            pltpu.VMEM((2, rows, width), BF16),
            half, half,
            pltpu.VMEM((2, -(-4 * tiles // 8) * 8, BLOCK), jnp.int32),
            table, table, table, table,
            block, block, block, half_block, half_block,
            pltpu.VMEM((2, tiles, XROWS, BLOCK), BF16),
            pltpu.VMEM((tiles, XROWS, BLOCK), F32),
            block,
            pltpu.VMEM((3, tiles, ZROWS, BLOCK), BF16),
            pltpu.VMEM((ZROWS, width), F32),
            pltpu.VMEM((ZROWS, width), F32),
            pltpu.VMEM((8, width), F32),
            pltpu.VMEM((tiles, rows, BLOCK), BF16),
            pltpu.VMEM((tiles, rows, BLOCK), BF16),
            half, half,
            pltpu.SemaphoreType.DMA((len(LOADS),)),
            pltpu.SemaphoreType.DMA((len(SENDS),)),
            pltpu.SemaphoreType.DMA((len(ARRIVALS),)),
        ],
        compiler_params=pltpu.CompilerParams(
            collective_id=0, has_side_effects=True, vmem_limit_bytes=32 * 2**20
        ),
        cost_estimate=pl.CostEstimate(flops=20_000_000, bytes_accessed=4_500_000, transcendentals=0),
    )(*[
        pltpu.with_memory_space_constraint(array, pltpu.HBM)
        for array in (local_params, base_params, momentum, encode_exponents, return_exponents)
    ])


def solution(mesh):
    return jax.shard_map(
        on_device,
        mesh=mesh,
        in_specs=(
            P("rep", None, "fsdp"),
            P(None, "fsdp"),
            P("rep", "fsdp"),
            P(None, "fsdp"),
            P(None, "fsdp"),
        ),
        out_specs=(P(None, "fsdp"), P("rep", "fsdp")),
        check_vma=False,
    )
```

```python
import jax
import jax.numpy as jnp
from jax import lax
from jax.experimental import pallas as pl
from jax.experimental.pallas import tpu as pltpu
from jax.sharding import PartitionSpec as P

BLOCK = 128
CODE_LIMIT = 448.0
MOMENTUM_RATE = 0.9
OUTER_RATE = 0.7
MESH = pl.DeviceIdType.MESH
BF16, F32 = jnp.bfloat16, jnp.float32
NX, NZ = 4, 4
ZROWS = 16
XROWS = NZ * ZROWS

ONE, TWO, ZFIRST = range(3)
CHUNKS = ((0, 3, ONE), (3, 6, ONE), (6, 9, TWO), (9, 11, ZFIRST))
BLOCKS, EXPONENTS, OTHER_BASE = 0, 4, 5
LOADS = 6
SWAP, SHARDS, SUMS, CODES, GATHER, CORE, MOMENT = range(7)
SENDS = 7
IN_SWAP, IN_MOMENT, IN_MOMENT_BACK, IN_CHUNKS = 0, 4, 5, 6
UP, DOWN, FIRST, SECOND, CODES_IN, NEAR_IN, FAR_IN, CORE_NEAR, CORE_FAR = range(9)
ARRIVALS = IN_CHUNKS + 9 * len(CHUNKS)
ENCODE, SEND_FAR, SEND_NEAR, JOIN, SUM, STEP, RING, LAND_NEAR, LAND, OWN, OWN_NEAR, OWN_FAR, OTHER_NEAR, OTHER_FAR = range(14)
SCHEDULE = (
    (SEND_FAR, 2), (ENCODE, 0), (ENCODE, 1), (SEND_NEAR, 2), (ENCODE, 3),
    (JOIN, 2), (SUM, 0), (SUM, 1), (SUM, 3), (SUM, 2),
    (STEP, 0), (STEP, 3), (STEP, 1), (STEP, 2), (RING, 0),
    (OWN, 0), (RING, 3), (RING, 1), (OWN, 1), (RING, 2),
    (OWN, 2), (LAND, 0), (OWN_FAR, 0), (LAND_NEAR, 0), (OWN_NEAR, 0),
    (OTHER_FAR, 0), (OTHER_NEAR, 0), (LAND, 1), (OWN_FAR, 1), (LAND_NEAR, 1),
    (LAND, 3), (OWN_NEAR, 1), (OWN_FAR, 3), (OTHER_FAR, 1), (OTHER_NEAR, 1),
    (OTHER_FAR, 3), (LAND, 2), (OWN_FAR, 2), (LAND_NEAR, 2), (OWN_NEAR, 2),
    (OTHER_FAR, 2), (OTHER_NEAR, 2),
)


def power_of_two(exponent):
    size = jnp.abs(exponent)
    result = jnp.ones(exponent.shape, F32)
    for bit in range(7):
        up, down = 2.0 ** (1 << bit), 2.0 ** -(1 << bit)
        factor = jnp.where(exponent < 0, down, up)
        result = result * jnp.where((size & (1 << bit)) != 0, factor, 1.0)
    return result


def kernel(
    params, base, momentum, enc_exp, ret_exp, new_params, new_momentum,
    exp_words, mine, sib_params, oth_base, exps, enc_mul, enc_scale, ret_mul, ret_scale,
    shards, up_in, down_in, x_in, z_in, t_wide, t_narrow, moment, moment_out, codes, sib_codes,
    load_sem, send_sem, recv_sem,
):
    rep = lax.axis_index("rep")
    x, z, c = rep // (NZ * 2), (rep // 2) % NZ, rep % 2
    width = sib_params.shape[1]
    tiles = width // BLOCK

    def place(px, pz, pc):
        return {"rep": (px * NZ + pz) * 2 + pc}

    sibling = place(x, z, 1 - c)
    right, far, left = (x + 1) % NX, (x + 2) % NX, (x + 3) % NX
    x_devs = [place((x + d) % NX, z, c) for d in (1, 2, 3)]
    z_devs = [place(x, (z + d) % NZ, c) for d in (1, 2, 3)]

    def rows_of(block):
        return pl.ds(pl.multiple_of(block * XROWS, XROWS), XROWS)

    own_cols = pl.ds(pl.multiple_of(c * width, BLOCK), width)
    oth_cols = pl.ds(pl.multiple_of((1 - c) * width, BLOCK), width)

    def local(src, dst, sem):
        pltpu.make_async_copy(src, dst, load_sem.at[sem]).start()

    def remote(src, dst, device, send, arrival):
        pltpu.make_async_remote_copy(
            src_ref=src, dst_ref=dst, send_sem=send_sem.at[send], recv_sem=recv_sem.at[arrival],
            device_id=device, device_id_type=MESH,
        ).start()

    def take(sem, ref):
        pltpu.make_async_copy(ref, ref, sem).wait()

    def loaded(sem, ref):
        take(load_sem.at[sem], ref)

    def arrived(sem, ref):
        take(recv_sem.at[sem], ref)

    def sent(sem, ref):
        take(send_sem.at[sem], ref)

    barrier = pltpu.get_barrier_semaphore()
    for device in x_devs + z_devs + [sibling]:
        pl.semaphore_signal(barrier, inc=1, device_id=device, device_id_type=MESH)

    order = (far, right, left, x)
    local(enc_exp, exp_words.at[0], EXPONENTS)
    local(ret_exp, exp_words.at[1], EXPONENTS)
    for which, block in enumerate(order):
        rows = rows_of(block)
        local(base.at[rows, own_cols], mine.at[0, rows], BLOCKS + which)
        local(params.at[0, rows, own_cols], mine.at[1, rows], BLOCKS + which)

    pl.semaphore_wait(barrier, 7)

    for which, block in enumerate(order):
        rows = rows_of(block)
        remote(params.at[0, rows, oth_cols], sib_params.at[rows], sibling, SWAP, IN_SWAP + which)
    moment_rows = pl.ds(pl.multiple_of(c * 8, 8), 8)
    other_rows = pl.ds(pl.multiple_of((1 - c) * 8, 8), 8)
    remote(momentum.at[:, oth_cols], moment.at[moment_rows], sibling, MOMENT, IN_MOMENT)
    pltpu.make_async_copy(momentum.at[:, own_cols], moment.at[moment_rows], recv_sem.at[IN_MOMENT]).start()
    local(base.at[:, oth_cols], oth_base, OTHER_BASE)

    loaded(EXPONENTS, exp_words)
    for half in range(2):
        for row in range(2):
            for tile in range(tiles):
                at = (half * 2 + row) * tiles + tile
                column = tile + (c if half == 0 else 1 - c) * tiles
                if half == 0:
                    exps[0, pl.ds(at, 1), :] = jnp.full((1, BLOCK), exp_words[0, row, column], jnp.int32)
                exps[1, pl.ds(at, 1), :] = jnp.full((1, BLOCK), exp_words[1, row, column], jnp.int32)
    encode_exps = exps[0, 0:2 * tiles, :]
    enc_mul[0:2 * tiles, :] = power_of_two(-encode_exps)
    later_tables = []

    def return_tables():
        if not later_tables:
            later_tables.append(True)
            return_exps = exps[1, 0:4 * tiles, :]
            enc_scale[0:2 * tiles, :] = power_of_two(exps[0, 0:2 * tiles, :]) * (1.0 / (2 * NX * NZ))
            ret_mul[0:4 * tiles, :] = power_of_two(-return_exps)
            ret_scale[0:4 * tiles, :] = power_of_two(return_exps)

    ready = set()

    def need(*blocks):
        for which in blocks:
            if which not in ready:
                ready.add(which)
                rows = rows_of(order[which])
                loaded(BLOCKS + which, mine.at[:, rows])
                arrived(IN_SWAP + which, sib_params.at[rows])

    def encoded_pair(which, tile):
        block = order[which]
        rows = rows_of(block)
        lanes = slice(tile * BLOCK, (tile + 1) * BLOCK)
        factor = enc_mul[pl.ds((block // 2) * tiles + tile, 1), :]
        start = mine[0, rows, lanes].astype(F32)
        total = None
        for source in (mine[1, rows, lanes], sib_params[rows, lanes]):
            code = jnp.clip((source.astype(F32) - start) * factor, -CODE_LIMIT, CODE_LIMIT)
            code = code.astype(BF16).astype(F32)
            total = code if total is None else total + code
        return total.reshape(NZ, ZROWS, BLOCK)

    def span(k):
        lo, hi, _ = CHUNKS[k]
        return range(lo, hi)

    def part(k):
        lo, hi, _ = CHUNKS[k]
        return pl.ds(lo, hi - lo)

    def mode(k):
        return CHUNKS[k][2]

    def event(k, what):
        return IN_CHUNKS + 9 * k + what

    def fill(which, k):
        for tile in span(k):
            shards[tile, order[which]] = encoded_pair(which, tile).astype(BF16)

    def encode(k):
        need(0, 1, 2)
        if mode(k) == ONE:
            for which, d in ((0, 2), (1, 1), (2, 3)):
                fill(which, k)
                remote(
                    shards.at[part(k), order[which]], x_in.at[d - 1, part(k)], x_devs[d - 1], SHARDS, event(k, FIRST)
                )
        else:
            need(3)
            for which in range(4):
                fill(which, k)
            for d in (2, 1, 3):
                remote(
                    shards.at[part(k), :, (z + d) % NZ], z_in.at[d - 1, part(k)], z_devs[d - 1], SHARDS, event(k, FIRST)
                )

    upper, lower = pl.ds(0, NZ // 2), pl.ds(NZ // 2, NZ // 2)

    def send_far(k):
        need(0)
        fill(0, k)
        remote(shards.at[part(k), far, upper], up_in.at[part(k)], x_devs[0], SHARDS, event(k, UP))
        remote(shards.at[part(k), far, lower], down_in.at[part(k)], x_devs[2], SHARDS, event(k, DOWN))

    def send_near(k):
        need(1, 2)
        fill(1, k)
        remote(shards.at[part(k), right, lower], x_in.at[0, part(k), lower], x_devs[0], SHARDS, event(k, FIRST))
        fill(2, k)
        remote(shards.at[part(k), left, upper], x_in.at[2, part(k), upper], x_devs[2], SHARDS, event(k, FIRST))

    def join(k):
        arrived(event(k, UP), up_in.at[part(k)])
        for tile in span(k):
            shards[tile, right, upper] = (shards[tile, right, upper].astype(F32) + up_in[tile].astype(F32)).astype(BF16)
        remote(shards.at[part(k), right, upper], x_in.at[0, part(k), upper], x_devs[0], SHARDS, event(k, FIRST))
        arrived(event(k, DOWN), down_in.at[part(k)])
        for tile in span(k):
            shards[tile, left, lower] = (shards[tile, left, lower].astype(F32) + down_in[tile].astype(F32)).astype(BF16)
        remote(shards.at[part(k), left, lower], x_in.at[2, part(k), lower], x_devs[2], SHARDS, event(k, FIRST))

    def sum_first(k):
        if mode(k) == ZFIRST:
            arrived(event(k, FIRST), z_in.at[:, part(k)])
        else:
            need(3)
            arrived(event(k, FIRST), x_in.at[pl.ds(0, 3 if mode(k) == ONE else 2), part(k)])
        for tile in span(k):
            if mode(k) == ZFIRST:
                total = shards[tile, :, z].astype(F32)
                parts = [z_in[d, tile] for d in range(3)]
            else:
                total = encoded_pair(3, tile)
                parts = [x_in[d, tile] for d in ((0, 1, 2) if mode(k) == ONE else (0, 2))]
            for piece in parts:
                total = total + piece.astype(F32)
            t_wide[tile] = total
            t_narrow[tile] = total.astype(BF16)
        for d in (2, 1, 3):
            if mode(k) == ZFIRST:
                remote(
                    t_narrow.at[part(k), (x + d) % NX], x_in.at[d - 1, part(k), 0], x_devs[d - 1], SUMS, event(k, SECOND)
                )
            else:
                remote(
                    t_narrow.at[part(k), (z + d) % NZ], z_in.at[d - 1, part(k), 0], z_devs[d - 1], SUMS, event(k, SECOND)
                )

    started = set()

    def step(k):
        return_tables()
        if not started:
            started.add(True)
            arrived(IN_MOMENT, moment)
        second = x_in if mode(k) == ZFIRST else z_in
        mine_at = x if mode(k) == ZFIRST else z
        arrived(event(k, SECOND), second.at[:, part(k), 0])
        for tile in span(k):
            lanes = slice(tile * BLOCK, (tile + 1) * BLOCK)
            at = pl.ds((x // 2) * tiles + tile, 1)
            summed = t_wide[tile, mine_at]
            for d in range(3):
                summed = summed + second[d, tile, 0].astype(F32)
            outer_grad = summed * enc_scale[at, :]
            new_moment = MOMENTUM_RATE * moment[:, lanes] + outer_grad
            moment_out[:, lanes] = new_moment
            outer_step = OUTER_RATE * (outer_grad + MOMENTUM_RATE * new_moment)
            code = jnp.clip(outer_step * ret_mul[at, :], -CODE_LIMIT, CODE_LIMIT)
            codes[tile, x, z] = code.astype(BF16)
        piece = codes.at[part(k), x, z]
        for d in (2, 1, 3):
            device = x_devs[d - 1] if mode(k) == ZFIRST else z_devs[d - 1]
            remote(piece, piece, device, CODES, event(k, CODES_IN))

    def to_sibling(k, block, arrival):
        remote(codes.at[part(k), block], sib_codes.at[part(k), block], sibling, CORE, event(k, arrival))

    def ring(k):
        arrived(event(k, CODES_IN), z_in.at[:, part(k), 0])
        if mode(k) == ZFIRST:
            piece = codes.at[part(k), :, z]
            for d in (2, 1, 3):
                remote(piece, piece, z_devs[d - 1], GATHER, event(k, FAR_IN))
        else:
            piece = codes.at[part(k), x]
            for d in (2, 1, 3):
                remote(piece, piece, x_devs[d - 1], GATHER, event(k, FAR_IN if d == 2 else NEAR_IN))
            to_sibling(k, x, CORE_NEAR)

    def land_near(k):
        arrived(event(k, NEAR_IN), codes.at[part(k), pl.ds(0, 2)])
        to_sibling(k, right, CORE_NEAR)
        to_sibling(k, left, CORE_NEAR)

    def land(k):
        if mode(k) == ZFIRST:
            arrived(event(k, FAR_IN), codes.at[part(k), pl.ds(0, 3)])
            remote(codes.at[part(k)], sib_codes.at[part(k)], sibling, CORE, event(k, CORE_FAR))
        else:
            arrived(event(k, FAR_IN), codes.at[part(k), 0])
            to_sibling(k, far, CORE_FAR)

    def apply(k, block, own):
        rows = rows_of(block)
        if not own and OTHER_BASE not in started:
            started.add(OTHER_BASE)
            loaded(OTHER_BASE, oth_base)
        for tile in span(k):
            lanes = slice(tile * BLOCK, (tile + 1) * BLOCK)
            at = pl.ds(((0 if own else 2) + block // 2) * tiles + tile, 1)
            code = (codes if own else sib_codes)[tile, block].reshape(XROWS, BLOCK).astype(F32)
            start = mine[0, rows, lanes] if own else oth_base[rows, lanes]
            out_lanes = pl.ds(pl.multiple_of((c if own else 1 - c) * width + tile * BLOCK, BLOCK), BLOCK)
            new_params[rows, out_lanes] = (start.astype(F32) + code * ret_scale[at, :]).astype(BF16)

    def own(k):
        apply(k, x, True)

    def own_near(k):
        apply(k, right, True)
        apply(k, left, True)

    def own_far(k):
        for block in order if mode(k) == ZFIRST else (far,):
            apply(k, block, True)

    def other_near(k):
        arrived(event(k, CORE_NEAR), codes.at[part(k), pl.ds(0, 3)])
        for block in (x, right, left):
            apply(k, block, False)

    def other_far(k):
        arrived(event(k, CORE_FAR), codes.at[part(k)] if mode(k) == ZFIRST else codes.at[part(k), 0])
        for block in order if mode(k) == ZFIRST else (far,):
            apply(k, block, False)

    stages = {
        ENCODE: encode, SEND_FAR: send_far, SEND_NEAR: send_near, JOIN: join, SUM: sum_first, STEP: step, RING: ring,
        LAND_NEAR: land_near, LAND: land, OWN: own, OWN_NEAR: own_near, OWN_FAR: own_far,
        OTHER_NEAR: other_near, OTHER_FAR: other_far,
    }
    steps_left = len(CHUNKS)
    for stage, k in SCHEDULE:
        stages[stage](k)
        if stage == STEP:
            steps_left -= 1
            if steps_left == 0:
                back = moment_out.at[other_rows]
                remote(back, new_momentum.at[:, own_cols], sibling, MOMENT, IN_MOMENT_BACK)
                new_momentum[:, own_cols] = moment_out[moment_rows]
    arrived(IN_MOMENT_BACK, new_momentum.at[:, oth_cols])

    sent(SWAP, sib_params)
    sent(SHARDS, shards.at[:, pl.ds(0, 3)])
    sent(SUMS, t_narrow.at[:, pl.ds(0, 3)])
    sent(CODES, t_narrow.at[:, pl.ds(0, 3)])
    sent(GATHER, codes.at[:, pl.ds(0, 3)])
    sent(CORE, codes)
    sent(MOMENT, moment)


def on_device(local_params, base_params, momentum, encode_exponents, return_exponents):
    _, rows, columns = local_params.shape
    width = columns // 2
    tiles = width // BLOCK
    table = pltpu.VMEM((-(-4 * tiles // 8) * 8, BLOCK), F32)
    half = pltpu.VMEM((rows, width), BF16)
    hbm = pl.BlockSpec(memory_space=pltpu.HBM)
    vmem = pl.BlockSpec(memory_space=pltpu.VMEM)
    return pl.pallas_call(
        kernel,
        name="outer_step",
        out_shape=(pltpu.VMEM((rows, columns), BF16), pltpu.VMEM(momentum.shape, F32)),
        in_specs=[hbm] * 5,
        out_specs=(vmem, vmem),
        scratch_shapes=[
            pltpu.SMEM((2,) + encode_exponents.shape, jnp.int32),
            pltpu.VMEM((2, rows, width), BF16),
            half, half,
            pltpu.VMEM((2, -(-4 * tiles // 8) * 8, BLOCK), jnp.int32),
            table, table, table, table,
            pltpu.VMEM((tiles, NX, NZ, ZROWS, BLOCK), BF16),
            pltpu.VMEM((tiles, NZ // 2, ZROWS, BLOCK), BF16),
            pltpu.VMEM((tiles, NZ // 2, ZROWS, BLOCK), BF16),
            pltpu.VMEM((3, tiles, NZ, ZROWS, BLOCK), BF16),
            pltpu.VMEM((3, tiles, NX, ZROWS, BLOCK), BF16),
            pltpu.VMEM((tiles, NZ, ZROWS, BLOCK), F32),
            pltpu.VMEM((tiles, NZ, ZROWS, BLOCK), BF16),
            pltpu.VMEM((ZROWS, width), F32),
            pltpu.VMEM((ZROWS, width), F32),
            pltpu.VMEM((tiles, NX, NZ, ZROWS, BLOCK), BF16),
            pltpu.VMEM((tiles, NX, NZ, ZROWS, BLOCK), BF16),
            pltpu.SemaphoreType.DMA((LOADS,)),
            pltpu.SemaphoreType.DMA((SENDS,)),
            pltpu.SemaphoreType.DMA((ARRIVALS,)),
        ],
        compiler_params=pltpu.CompilerParams(
            collective_id=0, has_side_effects=True, vmem_limit_bytes=32 * 2**20
        ),
        cost_estimate=pl.CostEstimate(flops=20_000_000, bytes_accessed=4_500_000, transcendentals=0),
    )(*[
        pltpu.with_memory_space_constraint(array, pltpu.HBM)
        for array in (local_params, base_params, momentum, encode_exponents, return_exponents)
    ])


def solution(mesh):
    return jax.shard_map(
        on_device,
        mesh=mesh,
        in_specs=(
            P("rep", None, "fsdp"),
            P(None, "fsdp"),
            P("rep", "fsdp"),
            P(None, "fsdp"),
            P(None, "fsdp"),
        ),
        out_specs=(P(None, "fsdp"), P("rep", "fsdp")),
        check_vma=False,
    )
```

```python
import jax
import jax.numpy as jnp
from jax import lax
from jax.experimental import pallas as pl
from jax.experimental.pallas import tpu as pltpu
from jax.sharding import PartitionSpec as P

BLOCK = 128
CODE_LIMIT = 448.0
MOMENTUM_RATE = 0.9
OUTER_RATE = 0.7
MESH = pl.DeviceIdType.MESH
BF16, F32 = jnp.bfloat16, jnp.float32
NX, NZ = 4, 4
ZROWS = 16
XROWS = NZ * ZROWS

ONE, TWO, ZFIRST = range(3)
CHUNKS = ((0, 4, TWO, ONE), (4, 8, TWO, ONE), (8, 11, ZFIRST, ONE))
BLOCKS, EXPONENTS, OTHER_BASE = 0, 4, 5
LOADS = 6
SWAP, SHARDS, SUMS, CODES, GATHER, CORE, MOMENT = range(7)
SENDS = 7
IN_SWAP, IN_MOMENT, IN_MOMENT_BACK, IN_CHUNKS = 0, 4, 5, 6
FIRST, SECOND, CODES_IN, FAR_IN, CORE_FAR, NEAR_IN, CORE_NEAR, UP, DOWN, RIGHTWARD, LEFTWARD = range(11)


def events():
    table = {}
    for k, (_, _, how, gather) in enumerate(CHUNKS):
        kinds = [FIRST, SECOND, CODES_IN, FAR_IN, CORE_FAR]
        kinds += [] if how == ZFIRST else [NEAR_IN, CORE_NEAR]
        kinds += [UP, DOWN] if how == TWO else []
        kinds += [RIGHTWARD, LEFTWARD] if gather == TWO else []
        for kind in kinds:
            table[k, kind] = IN_CHUNKS + len(table)
    return table


EVENTS = events()
ARRIVALS = IN_CHUNKS + len(EVENTS)
(
    ENCODE, SEND_FAR, SEND_NEAR, JOIN, PAIR, SUM, STEP, RING, PASS, LAND_NEAR, LAND,
    OWN, OWN_NEAR, OWN_FAR, OTHER_NEAR, OTHER_FAR,
) = range(16)
SCHEDULE = (
    (SEND_FAR, 0), (SEND_FAR, 1), (SEND_NEAR, 0), (SEND_NEAR, 1), (ENCODE, 2),
    (PAIR, 0), (PAIR, 1), (JOIN, 0), (JOIN, 1), (SUM, 0),
    (SUM, 1), (SUM, 2), (STEP, 0), (STEP, 2), (STEP, 1),
    (RING, 2), (RING, 0), (OWN, 0), (RING, 1), (OWN, 1),
    (LAND, 0), (OWN_FAR, 0), (LAND_NEAR, 0), (OWN_NEAR, 0), (OTHER_FAR, 0),
    (OTHER_NEAR, 0), (LAND, 1), (OWN_FAR, 1), (LAND, 2), (OWN_FAR, 2),
    (LAND_NEAR, 1), (OWN_NEAR, 1), (OTHER_FAR, 1), (OTHER_FAR, 2), (OTHER_NEAR, 1),
)


def power_of_two(exponent):
    size = jnp.abs(exponent)
    result = jnp.ones(exponent.shape, F32)
    for bit in range(7):
        up, down = 2.0 ** (1 << bit), 2.0 ** -(1 << bit)
        factor = jnp.where(exponent < 0, down, up)
        result = result * jnp.where((size & (1 << bit)) != 0, factor, 1.0)
    return result


def kernel(
    params, base, momentum, enc_exp, ret_exp, new_params, new_momentum,
    exp_words, mine, sib_params, oth_base, exps, enc_mul, enc_scale, ret_mul, ret_scale,
    shards, up_in, down_in, x_in, z_in, t_wide, t_narrow, moment, moment_out, codes, sib_codes,
    load_sem, send_sem, recv_sem,
):
    rep = lax.axis_index("rep")
    x, z, c = rep // (NZ * 2), (rep // 2) % NZ, rep % 2
    width = sib_params.shape[1]
    tiles = width // BLOCK

    def place(px, pz, pc):
        return {"rep": (px * NZ + pz) * 2 + pc}

    sibling = place(x, z, 1 - c)
    right, far, left = (x + 1) % NX, (x + 2) % NX, (x + 3) % NX
    x_devs = [place((x + d) % NX, z, c) for d in (1, 2, 3)]
    z_devs = [place(x, (z + d) % NZ, c) for d in (1, 2, 3)]

    def rows_of(block):
        return pl.ds(pl.multiple_of(block * XROWS, XROWS), XROWS)

    own_cols = pl.ds(pl.multiple_of(c * width, BLOCK), width)
    oth_cols = pl.ds(pl.multiple_of((1 - c) * width, BLOCK), width)

    def local(src, dst, sem):
        pltpu.make_async_copy(src, dst, load_sem.at[sem]).start()

    def remote(src, dst, device, send, arrival):
        pltpu.make_async_remote_copy(
            src_ref=src, dst_ref=dst, send_sem=send_sem.at[send], recv_sem=recv_sem.at[arrival],
            device_id=device, device_id_type=MESH,
        ).start()

    def take(sem, ref):
        pltpu.make_async_copy(ref, ref, sem).wait()

    def loaded(sem, ref):
        take(load_sem.at[sem], ref)

    def arrived(sem, ref):
        take(recv_sem.at[sem], ref)

    def sent(sem, ref):
        take(send_sem.at[sem], ref)

    barrier = pltpu.get_barrier_semaphore()
    for device in x_devs + z_devs + [sibling]:
        pl.semaphore_signal(barrier, inc=1, device_id=device, device_id_type=MESH)

    order = (far, right, left, x)
    local(enc_exp, exp_words.at[0], EXPONENTS)
    local(ret_exp, exp_words.at[1], EXPONENTS)
    for which, block in enumerate(order):
        rows = rows_of(block)
        local(base.at[rows, own_cols], mine.at[0, rows], BLOCKS + which)
        local(params.at[0, rows, own_cols], mine.at[1, rows], BLOCKS + which)

    pl.semaphore_wait(barrier, 7)

    for which, block in enumerate(order):
        rows = rows_of(block)
        remote(params.at[0, rows, oth_cols], sib_params.at[rows], sibling, SWAP, IN_SWAP + which)
    moment_rows = pl.ds(pl.multiple_of(c * 8, 8), 8)
    other_rows = pl.ds(pl.multiple_of((1 - c) * 8, 8), 8)
    remote(momentum.at[:, oth_cols], moment.at[moment_rows], sibling, MOMENT, IN_MOMENT)
    pltpu.make_async_copy(momentum.at[:, own_cols], moment.at[moment_rows], recv_sem.at[IN_MOMENT]).start()
    local(base.at[:, oth_cols], oth_base, OTHER_BASE)

    loaded(EXPONENTS, exp_words)
    for half in range(2):
        for row in range(2):
            for tile in range(tiles):
                at = (half * 2 + row) * tiles + tile
                column = tile + (c if half == 0 else 1 - c) * tiles
                if half == 0:
                    exps[0, pl.ds(at, 1), :] = jnp.full((1, BLOCK), exp_words[0, row, column], jnp.int32)
                exps[1, pl.ds(at, 1), :] = jnp.full((1, BLOCK), exp_words[1, row, column], jnp.int32)
    encode_exps = exps[0, 0:2 * tiles, :]
    enc_mul[0:2 * tiles, :] = power_of_two(-encode_exps)
    later_tables = []

    def return_tables():
        if not later_tables:
            later_tables.append(True)
            return_exps = exps[1, 0:4 * tiles, :]
            enc_scale[0:2 * tiles, :] = power_of_two(exps[0, 0:2 * tiles, :]) * (1.0 / (2 * NX * NZ))
            ret_mul[0:4 * tiles, :] = power_of_two(-return_exps)
            ret_scale[0:4 * tiles, :] = power_of_two(return_exps)

    ready = set()

    def need(*blocks):
        for which in blocks:
            if which not in ready:
                ready.add(which)
                rows = rows_of(order[which])
                loaded(BLOCKS + which, mine.at[:, rows])
                arrived(IN_SWAP + which, sib_params.at[rows])

    def encoded_pair(which, tile):
        block = order[which]
        rows = rows_of(block)
        lanes = slice(tile * BLOCK, (tile + 1) * BLOCK)
        factor = enc_mul[pl.ds((block // 2) * tiles + tile, 1), :]
        start = mine[0, rows, lanes].astype(F32)
        total = None
        for source in (mine[1, rows, lanes], sib_params[rows, lanes]):
            code = jnp.clip((source.astype(F32) - start) * factor, -CODE_LIMIT, CODE_LIMIT)
            code = code.astype(BF16).astype(F32)
            total = code if total is None else total + code
        return total.reshape(NZ, ZROWS, BLOCK)

    def span(k):
        lo, hi = CHUNKS[k][:2]
        return range(lo, hi)

    def part(k):
        lo, hi = CHUNKS[k][:2]
        return pl.ds(lo, hi - lo)

    def mode(k):
        return CHUNKS[k][2]

    def event(k, what):
        return EVENTS[k, what]

    def fill(which, k):
        for tile in span(k):
            shards[tile, order[which]] = encoded_pair(which, tile).astype(BF16)

    def encode(k):
        need(0, 1, 2)
        if mode(k) == ONE:
            for which, d in ((0, 2), (1, 1), (2, 3)):
                fill(which, k)
                remote(
                    shards.at[part(k), order[which]], x_in.at[d - 1, part(k)], x_devs[d - 1], SHARDS, event(k, FIRST)
                )
        else:
            need(3)
            for which in range(4):
                fill(which, k)
            for d in (2, 1, 3):
                remote(
                    shards.at[part(k), :, (z + d) % NZ], z_in.at[d - 1, part(k)], z_devs[d - 1], SHARDS, event(k, FIRST)
                )

    upper, lower = pl.ds(0, NZ // 2), pl.ds(NZ // 2, NZ // 2)

    def send_far(k):
        need(0)
        fill(0, k)
        remote(shards.at[part(k), far, upper], up_in.at[part(k)], x_devs[0], SHARDS, event(k, UP))
        remote(shards.at[part(k), far, lower], down_in.at[part(k)], x_devs[2], SHARDS, event(k, DOWN))

    def send_near(k):
        need(1, 2)
        fill(1, k)
        remote(shards.at[part(k), right, lower], x_in.at[0, part(k), lower], x_devs[0], SHARDS, event(k, FIRST))
        fill(2, k)
        remote(shards.at[part(k), left, upper], x_in.at[2, part(k), upper], x_devs[2], SHARDS, event(k, FIRST))

    def join(k):
        arrived(event(k, UP), up_in.at[part(k)])
        for tile in span(k):
            shards[tile, right, upper] = (shards[tile, right, upper].astype(F32) + up_in[tile].astype(F32)).astype(BF16)
        remote(shards.at[part(k), right, upper], x_in.at[0, part(k), upper], x_devs[0], SHARDS, event(k, FIRST))
        arrived(event(k, DOWN), down_in.at[part(k)])
        for tile in span(k):
            shards[tile, left, lower] = (shards[tile, left, lower].astype(F32) + down_in[tile].astype(F32)).astype(BF16)
        remote(shards.at[part(k), left, lower], x_in.at[2, part(k), lower], x_devs[2], SHARDS, event(k, FIRST))

    def pair(k):
        need(3)
        for tile in span(k):
            t_wide[tile] = encoded_pair(3, tile)

    def sum_first(k):
        if mode(k) == ZFIRST:
            arrived(event(k, FIRST), z_in.at[:, part(k)])
        else:
            arrived(event(k, FIRST), x_in.at[pl.ds(0, 3 if mode(k) == ONE else 2), part(k)])
        for tile in span(k):
            if mode(k) == ZFIRST:
                total = shards[tile, :, z].astype(F32)
                parts = [z_in[d, tile] for d in range(3)]
            else:
                total = t_wide[tile]
                parts = [x_in[d, tile] for d in ((0, 1, 2) if mode(k) == ONE else (0, 2))]
            for piece in parts:
                total = total + piece.astype(F32)
            t_wide[tile] = total
            t_narrow[tile] = total.astype(BF16)
        for d in (2, 1, 3):
            if mode(k) == ZFIRST:
                remote(
                    t_narrow.at[part(k), (x + d) % NX], x_in.at[d - 1, part(k), 0], x_devs[d - 1], SUMS, event(k, SECOND)
                )
            else:
                remote(
                    t_narrow.at[part(k), (z + d) % NZ], z_in.at[d - 1, part(k), 0], z_devs[d - 1], SUMS, event(k, SECOND)
                )

    started = set()

    def step(k):
        return_tables()
        if not started:
            started.add(True)
            arrived(IN_MOMENT, moment)
        second = x_in if mode(k) == ZFIRST else z_in
        mine_at = x if mode(k) == ZFIRST else z
        arrived(event(k, SECOND), second.at[:, part(k), 0])
        for tile in span(k):
            lanes = slice(tile * BLOCK, (tile + 1) * BLOCK)
            at = pl.ds((x // 2) * tiles + tile, 1)
            summed = t_wide[tile, mine_at]
            for d in range(3):
                summed = summed + second[d, tile, 0].astype(F32)
            outer_grad = summed * enc_scale[at, :]
            new_moment = MOMENTUM_RATE * moment[:, lanes] + outer_grad
            moment_out[:, lanes] = new_moment
            outer_step = OUTER_RATE * (outer_grad + MOMENTUM_RATE * new_moment)
            code = jnp.clip(outer_step * ret_mul[at, :], -CODE_LIMIT, CODE_LIMIT)
            codes[tile, x, z] = code.astype(BF16)
        piece = codes.at[part(k), x, z]
        for d in (2, 1, 3):
            device = x_devs[d - 1] if mode(k) == ZFIRST else z_devs[d - 1]
            remote(piece, piece, device, CODES, event(k, CODES_IN))

    def to_sibling(k, block, arrival):
        remote(codes.at[part(k), block], sib_codes.at[part(k), block], sibling, CORE, event(k, arrival))

    def ring(k):
        arrived(event(k, CODES_IN), z_in.at[:, part(k), 0])
        if mode(k) == ZFIRST:
            piece = codes.at[part(k), :, z]
            for d in (2, 1, 3):
                remote(piece, piece, z_devs[d - 1], GATHER, event(k, FAR_IN))
        elif CHUNKS[k][3] == ONE:
            piece = codes.at[part(k), x]
            for d in (2, 1, 3):
                remote(piece, piece, x_devs[d - 1], GATHER, event(k, FAR_IN if d == 2 else NEAR_IN))
            to_sibling(k, x, CORE_NEAR)
        else:
            first, second = codes.at[part(k), x, upper], codes.at[part(k), x, lower]
            remote(first, first, x_devs[0], GATHER, event(k, RIGHTWARD))
            remote(second, second, x_devs[2], GATHER, event(k, LEFTWARD))
            remote(second, second, x_devs[0], GATHER, event(k, NEAR_IN))
            remote(first, first, x_devs[2], GATHER, event(k, NEAR_IN))
            to_sibling(k, x, CORE_NEAR)

    def pass_on(k):
        first, second = codes.at[part(k), left, upper], codes.at[part(k), right, lower]
        arrived(event(k, RIGHTWARD), first)
        remote(first, first, x_devs[0], GATHER, event(k, FAR_IN))
        arrived(event(k, LEFTWARD), second)
        remote(second, second, x_devs[2], GATHER, event(k, FAR_IN))

    def land_near(k):
        arrived(event(k, NEAR_IN), codes.at[part(k), pl.ds(0, 2 if CHUNKS[k][3] == ONE else 1)])
        to_sibling(k, right, CORE_NEAR)
        to_sibling(k, left, CORE_NEAR)

    def land(k):
        if mode(k) == ZFIRST:
            arrived(event(k, FAR_IN), codes.at[part(k), pl.ds(0, 3)])
            remote(codes.at[part(k)], sib_codes.at[part(k)], sibling, CORE, event(k, CORE_FAR))
        else:
            arrived(event(k, FAR_IN), codes.at[part(k), 0])
            to_sibling(k, far, CORE_FAR)

    def apply(k, block, own):
        rows = rows_of(block)
        if not own and OTHER_BASE not in started:
            started.add(OTHER_BASE)
            loaded(OTHER_BASE, oth_base)
        for tile in span(k):
            lanes = slice(tile * BLOCK, (tile + 1) * BLOCK)
            at = pl.ds(((0 if own else 2) + block // 2) * tiles + tile, 1)
            code = (codes if own else sib_codes)[tile, block].reshape(XROWS, BLOCK).astype(F32)
            start = mine[0, rows, lanes] if own else oth_base[rows, lanes]
            out_lanes = pl.ds(pl.multiple_of((c if own else 1 - c) * width + tile * BLOCK, BLOCK), BLOCK)
            new_params[rows, out_lanes] = (start.astype(F32) + code * ret_scale[at, :]).astype(BF16)

    def own(k):
        apply(k, x, True)

    def own_near(k):
        apply(k, right, True)
        apply(k, left, True)

    def own_far(k):
        for block in order if mode(k) == ZFIRST else (far,):
            apply(k, block, True)

    def other_near(k):
        arrived(event(k, CORE_NEAR), codes.at[part(k), pl.ds(0, 3)])
        for block in (x, right, left):
            apply(k, block, False)

    def other_far(k):
        arrived(event(k, CORE_FAR), codes.at[part(k)] if mode(k) == ZFIRST else codes.at[part(k), 0])
        for block in order if mode(k) == ZFIRST else (far,):
            apply(k, block, False)

    stages = {
        ENCODE: encode, SEND_FAR: send_far, SEND_NEAR: send_near, JOIN: join, PAIR: pair, SUM: sum_first,
        STEP: step, RING: ring, PASS: pass_on,
        LAND_NEAR: land_near, LAND: land, OWN: own, OWN_NEAR: own_near, OWN_FAR: own_far,
        OTHER_NEAR: other_near, OTHER_FAR: other_far,
    }
    steps_left = len(CHUNKS)
    for stage, k in SCHEDULE:
        stages[stage](k)
        if stage == STEP:
            steps_left -= 1
            if steps_left == 0:
                back = moment_out.at[other_rows]
                remote(back, new_momentum.at[:, own_cols], sibling, MOMENT, IN_MOMENT_BACK)
                new_momentum[:, own_cols] = moment_out[moment_rows]
    arrived(IN_MOMENT_BACK, new_momentum.at[:, oth_cols])

    sent(SWAP, sib_params)
    sent(SHARDS, shards.at[:, pl.ds(0, 3)])
    sent(SUMS, t_narrow.at[:, pl.ds(0, 3)])
    sent(CODES, t_narrow.at[:, pl.ds(0, 3)])
    sent(GATHER, codes.at[:, pl.ds(0, 3)])
    sent(CORE, codes)
    sent(MOMENT, moment)


def store(params, momentum, params_out, momentum_out, sem):
    copies = [
        pltpu.make_async_copy(params, params_out, sem.at[0]), pltpu.make_async_copy(momentum, momentum_out, sem.at[1])
    ]
    for copy in copies:
        copy.start()
    for copy in copies:
        copy.wait()


def on_device(local_params, base_params, momentum, encode_exponents, return_exponents):
    _, rows, columns = local_params.shape
    width = columns // 2
    tiles = width // BLOCK
    table = pltpu.VMEM((-(-4 * tiles // 8) * 8, BLOCK), F32)
    half = pltpu.VMEM((rows, width), BF16)
    hbm = pl.BlockSpec(memory_space=pltpu.HBM)
    vmem = pl.BlockSpec(memory_space=pltpu.VMEM)
    held = pl.pallas_call(
        kernel,
        name="outer_step",
        out_shape=(pltpu.VMEM((rows, columns), BF16), pltpu.VMEM(momentum.shape, F32)),
        in_specs=[hbm] * 5,
        out_specs=(vmem, vmem),
        scratch_shapes=[
            pltpu.SMEM((2,) + encode_exponents.shape, jnp.int32),
            pltpu.VMEM((2, rows, width), BF16),
            half, half,
            pltpu.VMEM((2, -(-4 * tiles // 8) * 8, BLOCK), jnp.int32),
            table, table, table, table,
            pltpu.VMEM((tiles, NX, NZ, ZROWS, BLOCK), BF16),
            pltpu.VMEM((tiles, NZ // 2, ZROWS, BLOCK), BF16),
            pltpu.VMEM((tiles, NZ // 2, ZROWS, BLOCK), BF16),
            pltpu.VMEM((3, tiles, NZ, ZROWS, BLOCK), BF16),
            pltpu.VMEM((3, tiles, NX, ZROWS, BLOCK), BF16),
            pltpu.VMEM((tiles, NZ, ZROWS, BLOCK), F32),
            pltpu.VMEM((tiles, NZ, ZROWS, BLOCK), BF16),
            pltpu.VMEM((ZROWS, width), F32),
            pltpu.VMEM((ZROWS, width), F32),
            pltpu.VMEM((tiles, NX, NZ, ZROWS, BLOCK), BF16),
            pltpu.VMEM((tiles, NX, NZ, ZROWS, BLOCK), BF16),
            pltpu.SemaphoreType.DMA((LOADS,)),
            pltpu.SemaphoreType.DMA((SENDS,)),
            pltpu.SemaphoreType.DMA((ARRIVALS,)),
        ],
        compiler_params=pltpu.CompilerParams(
            collective_id=0, has_side_effects=True, vmem_limit_bytes=32 * 2**20
        ),
        cost_estimate=pl.CostEstimate(flops=20_000_000, bytes_accessed=4_500_000, transcendentals=0),
    )(*[
        pltpu.with_memory_space_constraint(array, pltpu.HBM)
        for array in (local_params, base_params, momentum, encode_exponents, return_exponents)
    ])
    return pl.pallas_call(
        store,
        name="store",
        out_shape=tuple(pltpu.HBM(array.shape, array.dtype) for array in held),
        in_specs=[vmem, vmem],
        out_specs=(hbm, hbm),
        scratch_shapes=[pltpu.SemaphoreType.DMA((2,))],
    )(*[pltpu.with_memory_space_constraint(array, pltpu.VMEM) for array in held])


def solution(mesh):
    return jax.shard_map(
        on_device,
        mesh=mesh,
        in_specs=(
            P("rep", None, "fsdp"),
            P(None, "fsdp"),
            P("rep", "fsdp"),
            P(None, "fsdp"),
            P(None, "fsdp"),
        ),
        out_specs=(P(None, "fsdp"), P("rep", "fsdp")),
        check_vma=False,
    )
```

```python
import jax
import jax.numpy as jnp
from jax import lax
from jax.experimental import pallas as pl
from jax.experimental.pallas import tpu as pltpu
from jax.sharding import PartitionSpec as P

BLOCK = 128
CODE_LIMIT = 448.0
MOMENTUM_RATE = 0.9
OUTER_RATE = 0.7
MESH = pl.DeviceIdType.MESH
BF16, F32 = jnp.bfloat16, jnp.float32
NX, NZ = 4, 4
ZROWS = 16
XROWS = NZ * ZROWS

ONE, ZFIRST = range(2)
CHUNKS = ((0, 2, ONE), (2, 5, ONE), (5, 8, ONE), (8, 10, ZFIRST), (10, 11, ZFIRST))
BLOCKS, EXPONENTS, OTHER_BASE = 0, 5, 6
LOADS = 7
SWAP, SHARDS, SUMS, CODES, GATHER, CORE, MOMENT = range(7)
SENDS = 7
IN_SWAP, IN_MOMENT, IN_MOMENT_BACK, IN_CHUNKS = 0, 5, 6, 7
Z_TILE = min([lo for lo, _, how in CHUNKS if how == ZFIRST], default=0)
WHOLE = 4
FIRST, OWNED, SECOND, FAR_IN, CORE_FAR, CODES_IN, NEAR_IN, CORE_NEAR = 0, 1, 2, 3, 4, 5, 9, 10


def chunk_starts():
    starts = [IN_CHUNKS]
    for _, _, how in CHUNKS:
        starts.append(starts[-1] + (9 if how == ZFIRST else 11))
    return starts


STARTS = chunk_starts()
ARRIVALS = STARTS[-1]
(
    ENCODE, SEND_OWNED, PAIR, SUM, STEP, RING, LAND_NEAR, LAND, OWN, OWN_NEAR, OWN_FAR, OTHER_NEAR, OTHER_FAR,
) = range(13)
SCHEDULE = (
    (ENCODE, 0), (ENCODE, 1), (ENCODE, 2), (PAIR, 0), (PAIR, 1), (PAIR, 2),
    (ENCODE, 3), (ENCODE, 4), (SEND_OWNED, 0), (SEND_OWNED, 1), (SEND_OWNED, 2), (SEND_OWNED, 3),
    (SEND_OWNED, 4), (SUM, 0), (SUM, 1), (SUM, 3), (SUM, 2), (SUM, 4),
    (STEP, 0), (STEP, 1), (STEP, 3), (STEP, 4), (STEP, 2), (RING, 0),
    (OWN, 0), (RING, 3), (RING, 4), (RING, 1), (OWN, 1), (RING, 2),
    (OWN, 2), (LAND_NEAR, 0), (OWN_NEAR, 0), (LAND, 0), (OWN_FAR, 0), (OTHER_NEAR, 0),
    (OTHER_FAR, 0), (LAND_NEAR, 1), (LAND, 1), (OWN_NEAR, 1), (OWN_FAR, 1), (LAND, 3),
    (OWN_FAR, 3), (OTHER_NEAR, 1), (OTHER_FAR, 1), (LAND_NEAR, 2), (LAND, 2), (OWN_NEAR, 2),
    (LAND, 4), (OWN_FAR, 2), (OWN_FAR, 4), (OTHER_FAR, 3), (OTHER_NEAR, 2), (OTHER_FAR, 2),
    (OTHER_FAR, 4),
)


def power_of_two(exponent):
    size = jnp.abs(exponent)
    result = jnp.ones(exponent.shape, F32)
    for bit in range(7):
        up, down = 2.0 ** (1 << bit), 2.0 ** -(1 << bit)
        factor = jnp.where(exponent < 0, down, up)
        result = result * jnp.where((size & (1 << bit)) != 0, factor, 1.0)
    return result


def kernel(
    params, base, momentum, enc_exp, ret_exp, new_params, new_momentum,
    exp_words, mine, sib_params, oth_base, exps, enc_mul, enc_scale, ret_mul, ret_scale,
    shards, x_in, z_in, t_wide, t_narrow, moment, moment_out, codes, sib_codes,
    load_sem, send_sem, recv_sem,
):
    rep = lax.axis_index("rep")
    x, z, c = rep // (NZ * 2), (rep // 2) % NZ, rep % 2
    width = sib_params.shape[1]
    tiles = width // BLOCK

    def place(px, pz, pc):
        return {"rep": (px * NZ + pz) * 2 + pc}

    sibling = place(x, z, 1 - c)
    right, far, left = (x + 1) % NX, (x + 2) % NX, (x + 3) % NX
    x_devs = [place((x + d) % NX, z, c) for d in (1, 2, 3)]
    z_devs = [place(x, (z + d) % NZ, c) for d in (1, 2, 3)]

    def rows_of(block):
        return pl.ds(pl.multiple_of(block * XROWS, XROWS), XROWS)

    own_cols = pl.ds(pl.multiple_of(c * width, BLOCK), width)
    oth_cols = pl.ds(pl.multiple_of((1 - c) * width, BLOCK), width)

    def local(src, dst, sem):
        pltpu.make_async_copy(src, dst, load_sem.at[sem]).start()

    def remote(src, dst, device, send, arrival):
        pltpu.make_async_remote_copy(
            src_ref=src, dst_ref=dst, send_sem=send_sem.at[send], recv_sem=recv_sem.at[arrival],
            device_id=device, device_id_type=MESH,
        ).start()

    def take(sem, ref):
        pltpu.make_async_copy(ref, ref, sem).wait()

    def loaded(sem, ref):
        take(load_sem.at[sem], ref)

    def arrived(sem, ref):
        take(recv_sem.at[sem], ref)

    def sent(sem, ref):
        take(send_sem.at[sem], ref)

    barrier = pltpu.get_barrier_semaphore()
    for device in x_devs + z_devs + [sibling]:
        pl.semaphore_signal(barrier, inc=1, device_id=device, device_id_type=MESH)

    order = (far, right, left, x)
    first_z = Z_TILE * BLOCK

    def piece(which):
        if which == WHOLE:
            return pl.ds(0, NX * XROWS), first_z, width - first_z
        return rows_of(order[which]), 0, first_z

    def columns(core, first, count):
        return pl.ds(pl.multiple_of(core * width + first, BLOCK), count)

    pieces = (0, 1, 2, 3, WHOLE)
    for which in pieces:
        rows, first, count = piece(which)
        lanes = pl.ds(first, count)
        local(base.at[rows, columns(c, first, count)], mine.at[0, rows, lanes], BLOCKS + which)
        local(params.at[0, rows, columns(c, first, count)], mine.at[1, rows, lanes], BLOCKS + which)
    local(enc_exp, exp_words.at[0], EXPONENTS)
    local(ret_exp, exp_words.at[1], EXPONENTS)

    pl.semaphore_wait(barrier, 7)

    for which in pieces:
        rows, first, count = piece(which)
        remote(
            params.at[0, rows, columns(1 - c, first, count)], sib_params.at[rows, pl.ds(first, count)],
            sibling, SWAP, IN_SWAP + which,
        )
    moment_rows = pl.ds(pl.multiple_of(c * 8, 8), 8)
    other_rows = pl.ds(pl.multiple_of((1 - c) * 8, 8), 8)
    remote(momentum.at[:, oth_cols], moment.at[moment_rows], sibling, MOMENT, IN_MOMENT)
    pltpu.make_async_copy(momentum.at[:, own_cols], moment.at[moment_rows], recv_sem.at[IN_MOMENT]).start()
    local(base.at[:, oth_cols], oth_base, OTHER_BASE)

    loaded(EXPONENTS, exp_words)
    for half in range(2):
        for row in range(2):
            for tile in range(tiles):
                at = (half * 2 + row) * tiles + tile
                column = tile + (c if half == 0 else 1 - c) * tiles
                if half == 0:
                    exps[0, pl.ds(at, 1), :] = jnp.full((1, BLOCK), exp_words[0, row, column], jnp.int32)
                exps[1, pl.ds(at, 1), :] = jnp.full((1, BLOCK), exp_words[1, row, column], jnp.int32)
    encode_exps = exps[0, 0:2 * tiles, :]
    enc_mul[0:2 * tiles, :] = power_of_two(-encode_exps)
    later_tables = []

    def return_tables():
        if not later_tables:
            later_tables.append(True)
            return_exps = exps[1, 0:4 * tiles, :]
            enc_scale[0:2 * tiles, :] = power_of_two(exps[0, 0:2 * tiles, :]) * (1.0 / (2 * NX * NZ))
            ret_mul[0:4 * tiles, :] = power_of_two(-return_exps)
            ret_scale[0:4 * tiles, :] = power_of_two(return_exps)

    ready = set()

    def need(*blocks):
        for which in blocks:
            if which not in ready:
                ready.add(which)
                rows, first, count = piece(which)
                lanes = pl.ds(first, count)
                loaded(BLOCKS + which, mine.at[:, rows, lanes])
                arrived(IN_SWAP + which, sib_params.at[rows, lanes])

    def encoded_pair(which, tile):
        block = order[which]
        rows = rows_of(block)
        lanes = slice(tile * BLOCK, (tile + 1) * BLOCK)
        factor = enc_mul[pl.ds((block // 2) * tiles + tile, 1), :]
        start = mine[0, rows, lanes].astype(F32)
        total = None
        for source in (mine[1, rows, lanes], sib_params[rows, lanes]):
            code = jnp.clip((source.astype(F32) - start) * factor, -CODE_LIMIT, CODE_LIMIT)
            code = code.astype(BF16).astype(F32)
            total = code if total is None else total + code
        return total.reshape(NZ, ZROWS, BLOCK)

    def span(k):
        lo, hi = CHUNKS[k][:2]
        return range(lo, hi)

    def part(k):
        lo, hi = CHUNKS[k][:2]
        return pl.ds(lo, hi - lo)

    def mode(k):
        return CHUNKS[k][2]

    def event(k, what):
        return STARTS[k] + what

    def fill(which, k):
        for tile in span(k):
            shards[tile, order[which]] = encoded_pair(which, tile).astype(BF16)

    def encode(k):
        if mode(k) == ONE:
            need(0, 1, 2)
            for which, d in ((0, 2), (1, 1), (2, 3)):
                fill(which, k)
                for e in (2, 1, 3):
                    at = (z + e) % NZ
                    remote(
                        shards.at[part(k), order[which], at], x_in.at[d - 1, part(k), at], x_devs[d - 1],
                        SHARDS, event(k, FIRST),
                    )
        else:
            need(WHOLE)
            for which in range(4):
                fill(which, k)
            for d in (2, 1, 3):
                for e in (2, 1, 3):
                    at = (x + e) % NX
                    remote(
                        shards.at[part(k), at, (z + d) % NZ], z_in.at[d - 1, part(k), at], z_devs[d - 1],
                        SHARDS, event(k, FIRST),
                    )

    def send_owned(k):
        for d in (2, 1, 3):
            if mode(k) == ONE:
                remote(
                    shards.at[part(k), (x + d) % NX, z], x_in.at[d - 1, part(k), z], x_devs[d - 1],
                    SHARDS, event(k, OWNED),
                )
            else:
                remote(
                    shards.at[part(k), x, (z + d) % NZ], z_in.at[d - 1, part(k), x], z_devs[d - 1],
                    SHARDS, event(k, OWNED),
                )

    def pair(k):
        need(3)
        for tile in span(k):
            t_wide[tile] = encoded_pair(3, tile)

    def first_total(k, tile, at):
        if mode(k) == ONE:
            total, parts = t_wide[tile, at], x_in
        else:
            total, parts = shards[tile, at, z].astype(F32), z_in
        for d in range(3):
            total = total + parts[d, tile, at].astype(F32)
        return total

    def sum_first(k):
        arrived(event(k, FIRST), (x_in if mode(k) == ONE else z_in).at[:, part(k), pl.ds(0, 3)])
        for d in (2, 1, 3):
            at = ((z if mode(k) == ONE else x) + d) % NZ
            for tile in span(k):
                t_narrow[tile, at] = first_total(k, tile, at).astype(BF16)
            landing, devices = (z_in, z_devs) if mode(k) == ONE else (x_in, x_devs)
            remote(t_narrow.at[part(k), at], landing.at[d - 1, part(k), 0], devices[d - 1], SUMS, event(k, SECOND))

    started = set()

    def step(k):
        return_tables()
        if not started:
            started.add(True)
            arrived(IN_MOMENT, moment)
        second = x_in if mode(k) == ZFIRST else z_in
        mine_at = x if mode(k) == ZFIRST else z
        arrived(event(k, OWNED), second.at[:, part(k), 0])
        arrived(event(k, SECOND), second.at[:, part(k), 0])
        for tile in span(k):
            lanes = slice(tile * BLOCK, (tile + 1) * BLOCK)
            at = pl.ds((x // 2) * tiles + tile, 1)
            summed = first_total(k, tile, mine_at)
            for d in range(3):
                summed = summed + second[d, tile, 0].astype(F32)
            outer_grad = summed * enc_scale[at, :]
            new_moment = MOMENTUM_RATE * moment[:, lanes] + outer_grad
            moment_out[:, lanes] = new_moment
            outer_step = OUTER_RATE * (outer_grad + MOMENTUM_RATE * new_moment)
            code = jnp.clip(outer_step * ret_mul[at, :], -CODE_LIMIT, CODE_LIMIT)
            codes[tile, x, z] = code.astype(BF16)
        piece = codes.at[part(k), x, z]
        for d in (2, 1, 3):
            if mode(k) == ONE:
                remote(piece, piece, z_devs[d - 1], CODES, event(k, CODES_IN + z))
            else:
                remote(piece, piece, x_devs[d - 1], CODES, event(k, CODES_IN + x))
        gather(k, piece)

    def gather(k, piece):
        for d in (2, 1, 3):
            if mode(k) == ONE:
                remote(piece, piece, x_devs[d - 1], GATHER, event(k, FAR_IN if d == 2 else NEAR_IN))
            else:
                remote(piece, piece, z_devs[d - 1], GATHER, event(k, FAR_IN))

    def to_sibling(k, block, arrival):
        remote(codes.at[part(k), block], sib_codes.at[part(k), block], sibling, CORE, event(k, arrival))

    line_order = [jnp.where(z < 2, at, 3 - at) for at in (1 - jnp.minimum(z, 3 - z), 2, 3)]

    def ring(k):
        for at in line_order if mode(k) == ONE else (right, left, far):
            piece = codes.at[part(k), x, at] if mode(k) == ONE else codes.at[part(k), at, z]
            arrived(event(k, CODES_IN + at), piece)
            gather(k, piece)
        if mode(k) == ONE:
            to_sibling(k, x, CORE_NEAR)

    def land_near(k):
        arrived(event(k, NEAR_IN), codes.at[part(k), pl.ds(0, 2)])
        to_sibling(k, right, CORE_NEAR)
        to_sibling(k, left, CORE_NEAR)

    def land(k):
        if mode(k) == ZFIRST:
            arrived(event(k, FAR_IN), codes.at[part(k), pl.ds(0, 3)])
            remote(codes.at[part(k)], sib_codes.at[part(k)], sibling, CORE, event(k, CORE_FAR))
        else:
            arrived(event(k, FAR_IN), codes.at[part(k), 0])
            to_sibling(k, far, CORE_FAR)

    def apply(k, block, own):
        rows = rows_of(block)
        if not own and OTHER_BASE not in started:
            started.add(OTHER_BASE)
            loaded(OTHER_BASE, oth_base)
        for tile in span(k):
            lanes = slice(tile * BLOCK, (tile + 1) * BLOCK)
            at = pl.ds(((0 if own else 2) + block // 2) * tiles + tile, 1)
            code = (codes if own else sib_codes)[tile, block].reshape(XROWS, BLOCK).astype(F32)
            start = mine[0, rows, lanes] if own else oth_base[rows, lanes]
            out_lanes = pl.ds(pl.multiple_of((c if own else 1 - c) * width + tile * BLOCK, BLOCK), BLOCK)
            new_params[rows, out_lanes] = (start.astype(F32) + code * ret_scale[at, :]).astype(BF16)

    def own(k):
        apply(k, x, True)

    def own_near(k):
        apply(k, right, True)
        apply(k, left, True)

    def own_far(k):
        for block in order if mode(k) == ZFIRST else (far,):
            apply(k, block, True)

    def other_near(k):
        arrived(event(k, CORE_NEAR), codes.at[part(k), pl.ds(0, 3)])
        for block in (x, right, left):
            apply(k, block, False)

    def other_far(k):
        arrived(event(k, CORE_FAR), codes.at[part(k)] if mode(k) == ZFIRST else codes.at[part(k), 0])
        for block in order if mode(k) == ZFIRST else (far,):
            apply(k, block, False)

    stages = {
        ENCODE: encode, SEND_OWNED: send_owned, PAIR: pair, SUM: sum_first, STEP: step, RING: ring,
        LAND_NEAR: land_near, LAND: land, OWN: own, OWN_NEAR: own_near, OWN_FAR: own_far,
        OTHER_NEAR: other_near, OTHER_FAR: other_far,
    }
    steps_left = len(CHUNKS)
    for stage, k in SCHEDULE:
        stages[stage](k)
        if stage == STEP:
            steps_left -= 1
            if steps_left == 0:
                back = moment_out.at[other_rows]
                remote(back, new_momentum.at[:, own_cols], sibling, MOMENT, IN_MOMENT_BACK)
                new_momentum[:, own_cols] = moment_out[moment_rows]
    arrived(IN_MOMENT_BACK, new_momentum.at[:, oth_cols])

    sent(SWAP, sib_params)
    sent(SHARDS, shards.at[:, pl.ds(0, 3)])
    sent(SUMS, t_narrow.at[:, pl.ds(0, 3)])
    sent(CODES, t_narrow.at[:, pl.ds(0, 3)])
    sent(GATHER, codes.at[:, pl.ds(0, 3)])
    sent(CORE, codes)
    sent(MOMENT, moment)


def store(params, momentum, params_out, momentum_out, sem):
    copies = [
        pltpu.make_async_copy(params, params_out, sem.at[0]), pltpu.make_async_copy(momentum, momentum_out, sem.at[1])
    ]
    for copy in copies:
        copy.start()
    for copy in copies:
        copy.wait()


def on_device(local_params, base_params, momentum, encode_exponents, return_exponents):
    _, rows, columns = local_params.shape
    width = columns // 2
    tiles = width // BLOCK
    table = pltpu.VMEM((-(-4 * tiles // 8) * 8, BLOCK), F32)
    half = pltpu.VMEM((rows, width), BF16)
    hbm = pl.BlockSpec(memory_space=pltpu.HBM)
    vmem = pl.BlockSpec(memory_space=pltpu.VMEM)
    held = pl.pallas_call(
        kernel,
        name="outer_step",
        out_shape=(pltpu.VMEM((rows, columns), BF16), pltpu.VMEM(momentum.shape, F32)),
        in_specs=[hbm] * 5,
        out_specs=(vmem, vmem),
        scratch_shapes=[
            pltpu.SMEM((2,) + encode_exponents.shape, jnp.int32),
            pltpu.VMEM((2, rows, width), BF16),
            half, half,
            pltpu.VMEM((2, -(-4 * tiles // 8) * 8, BLOCK), jnp.int32),
            table, table, table, table,
            pltpu.VMEM((tiles, NX, NZ, ZROWS, BLOCK), BF16),
            pltpu.VMEM((3, tiles, NZ, ZROWS, BLOCK), BF16),
            pltpu.VMEM((3, tiles, NX, ZROWS, BLOCK), BF16),
            pltpu.VMEM((tiles, NZ, ZROWS, BLOCK), F32),
            pltpu.VMEM((tiles, NZ, ZROWS, BLOCK), BF16),
            pltpu.VMEM((ZROWS, width), F32),
            pltpu.VMEM((ZROWS, width), F32),
            pltpu.VMEM((tiles, NX, NZ, ZROWS, BLOCK), BF16),
            pltpu.VMEM((tiles, NX, NZ, ZROWS, BLOCK), BF16),
            pltpu.SemaphoreType.DMA((LOADS,)),
            pltpu.SemaphoreType.DMA((SENDS,)),
            pltpu.SemaphoreType.DMA((ARRIVALS,)),
        ],
        compiler_params=pltpu.CompilerParams(
            collective_id=0, has_side_effects=True, vmem_limit_bytes=32 * 2**20
        ),
        cost_estimate=pl.CostEstimate(flops=20_000_000, bytes_accessed=4_500_000, transcendentals=0),
    )(*[
        pltpu.with_memory_space_constraint(array, pltpu.HBM)
        for array in (local_params, base_params, momentum, encode_exponents, return_exponents)
    ])
    return pl.pallas_call(
        store,
        name="store",
        out_shape=tuple(pltpu.HBM(array.shape, array.dtype) for array in held),
        in_specs=[vmem, vmem],
        out_specs=(hbm, hbm),
        scratch_shapes=[pltpu.SemaphoreType.DMA((2,))],
    )(*[pltpu.with_memory_space_constraint(array, pltpu.VMEM) for array in held])


def solution(mesh):
    return jax.shard_map(
        on_device,
        mesh=mesh,
        in_specs=(
            P("rep", None, "fsdp"),
            P(None, "fsdp"),
            P("rep", "fsdp"),
            P(None, "fsdp"),
            P(None, "fsdp"),
        ),
        out_specs=(P(None, "fsdp"), P("rep", "fsdp")),
        check_vma=False,
    )
```

```python
import jax
import jax.numpy as jnp
from jax import lax
from jax.experimental import pallas as pl
from jax.experimental.pallas import tpu as pltpu
from jax.sharding import PartitionSpec as P

BLOCK = 128
CODE_LIMIT = 448.0
MOMENTUM_RATE = 0.9
OUTER_RATE = 0.7
MESH = pl.DeviceIdType.MESH
BF16, F32 = jnp.bfloat16, jnp.float32
NX, NZ = 4, 4
ZROWS = 16
XROWS = NZ * ZROWS

ONE, ZFIRST, BOTH = range(3)
CHUNKS = ((0, 3, ONE), (3, 6, ONE), (6, 8, BOTH), (8, 9, ZFIRST), (9, 11, ZFIRST))
EXPONENTS, OTHER_BASE = range(2)
LOADS = 2
SWAP, SHARDS, SUMS, CODES, GATHER, CORE, MOMENT, TWICE = range(8)
SENDS = 8
IN_SWAP, IN_MOMENT, IN_MOMENT_BACK, IN_CHUNKS = 0, 5, 6, 7
Z_TILE = min([lo for lo, _, how in CHUNKS if how == ZFIRST], default=0)
WHOLE = 4
FIRST, SECOND, FAR_IN, CORE_FAR, CODES_IN, NEAR_IN, CORE_NEAR = 0, 1, 2, 3, 4, 8, 9


def chunk_starts():
    starts = [IN_CHUNKS]
    for _, _, how in CHUNKS:
        starts.append(starts[-1] + (8 if how == ZFIRST else 10))
    return starts


STARTS = chunk_starts()
ARRIVALS = STARTS[-1]
(
    ENCODE, SEND_OWNED, PAIR, SUM, STEP, RING, LAND_NEAR, LAND, OWN, OWN_NEAR, OWN_FAR, OTHER_NEAR, OTHER_FAR,
) = range(13)
SCHEDULE = (
    (ENCODE, 0), (ENCODE, 1), (ENCODE, 2), (PAIR, 0), (PAIR, 1), (PAIR, 2),
    (ENCODE, 3), (ENCODE, 4), (SEND_OWNED, 0), (SEND_OWNED, 1), (SEND_OWNED, 2), (SEND_OWNED, 3),
    (SEND_OWNED, 4), (SUM, 0), (SUM, 3), (SUM, 1), (SUM, 2), (SUM, 4),
    (STEP, 3), (STEP, 0), (STEP, 1), (STEP, 4), (STEP, 2), (RING, 3),
    (RING, 0), (OWN, 0), (RING, 4), (RING, 1), (OWN, 1), (RING, 2),
    (OWN, 2), (LAND, 3), (OWN_FAR, 3), (OTHER_NEAR, 2), (LAND_NEAR, 0), (LAND, 0),
    (OWN_NEAR, 0), (OWN_FAR, 0), (OTHER_FAR, 3), (OTHER_NEAR, 0), (OTHER_FAR, 0), (LAND_NEAR, 1),
    (LAND, 1), (OWN_NEAR, 1), (OWN_FAR, 1), (LAND, 4), (OWN_FAR, 4), (OTHER_NEAR, 1),
    (OTHER_FAR, 1), (LAND, 2), (OTHER_FAR, 2), (OWN_FAR, 2), (LAND_NEAR, 2), (OWN_NEAR, 2),
    (OTHER_FAR, 4),
)


def power_of_two(exponent):
    size = jnp.abs(exponent)
    result = jnp.ones(exponent.shape, F32)
    for bit in range(7):
        up, down = 2.0 ** (1 << bit), 2.0 ** -(1 << bit)
        factor = jnp.where(exponent < 0, down, up)
        result = result * jnp.where((size & (1 << bit)) != 0, factor, 1.0)
    return result


def kernel(
    params, base, momentum, enc_exp, ret_exp, new_params, new_momentum,
    exp_words, mine, oth_base, exps, enc_mul, enc_scale, ret_mul, ret_scale,
    shards, x_in, z_in, t_wide, t_narrow, moment, moment_out, codes, sib_codes,
    load_sem, send_sem, recv_sem,
):
    rep = lax.axis_index("rep")
    x, z, c = rep // (NZ * 2), (rep // 2) % NZ, rep % 2
    width = mine.shape[2]
    tiles = width // BLOCK

    def place(px, pz, pc):
        return {"rep": (px * NZ + pz) * 2 + pc}

    sibling = place(x, z, 1 - c)
    right, far, left = (x + 1) % NX, (x + 2) % NX, (x + 3) % NX
    x_devs = [place((x + d) % NX, z, c) for d in (1, 2, 3)]
    z_devs = [place(x, (z + d) % NZ, c) for d in (1, 2, 3)]
    cross_devs = [place((x + d) % NX, z, 1 - c) for d in (1, 2, 3)]

    def rows_of(block):
        return pl.ds(pl.multiple_of(block * XROWS, XROWS), XROWS)

    own_cols = pl.ds(pl.multiple_of(c * width, BLOCK), width)
    oth_cols = pl.ds(pl.multiple_of((1 - c) * width, BLOCK), width)

    def local(src, dst, sem):
        pltpu.make_async_copy(src, dst, load_sem.at[sem]).start()

    def beside_swap(src, dst, arrival):
        pltpu.make_async_copy(src, dst, recv_sem.at[arrival]).start()

    def remote(src, dst, device, send, arrival):
        pltpu.make_async_remote_copy(
            src_ref=src, dst_ref=dst, send_sem=send_sem.at[send], recv_sem=recv_sem.at[arrival],
            device_id=device, device_id_type=MESH,
        ).start()

    def take(sem, ref):
        pltpu.make_async_copy(ref, ref, sem).wait()

    def loaded(sem, ref):
        take(load_sem.at[sem], ref)

    def arrived(sem, ref):
        take(recv_sem.at[sem], ref)

    def sent(sem, ref):
        take(send_sem.at[sem], ref)

    barrier = pltpu.get_barrier_semaphore()
    for device in x_devs + z_devs + cross_devs + [sibling]:
        pl.semaphore_signal(barrier, inc=1, device_id=device, device_id_type=MESH)

    order = (far, right, left, x)
    first_z = Z_TILE * BLOCK

    def piece(which):
        if which == WHOLE:
            return pl.ds(0, NX * XROWS), first_z, width - first_z
        return rows_of(order[which]), 0, first_z

    def columns(core, first, count):
        return pl.ds(pl.multiple_of(core * width + first, BLOCK), count)

    pieces = (0, 1, 2, 3, WHOLE)
    for which in pieces:
        rows, first, count = piece(which)
        lanes = pl.ds(first, count)
        beside_swap(base.at[rows, columns(c, first, count)], mine.at[0, rows, lanes], IN_SWAP + which)
        beside_swap(params.at[0, rows, columns(c, first, count)], mine.at[1, rows, lanes], IN_SWAP + which)
    local(enc_exp, exp_words.at[0], EXPONENTS)
    local(ret_exp, exp_words.at[1], EXPONENTS)

    pl.semaphore_wait(barrier, 10)

    for which in pieces:
        rows, first, count = piece(which)
        remote(
            params.at[0, rows, columns(1 - c, first, count)], mine.at[2, rows, pl.ds(first, count)],
            sibling, SWAP, IN_SWAP + which,
        )
    moment_rows = pl.ds(pl.multiple_of(c * 8, 8), 8)
    other_rows = pl.ds(pl.multiple_of((1 - c) * 8, 8), 8)
    remote(momentum.at[:, oth_cols], moment.at[moment_rows], sibling, MOMENT, IN_MOMENT)
    beside_swap(momentum.at[:, own_cols], moment.at[moment_rows], IN_MOMENT)
    local(base.at[:, oth_cols], oth_base, OTHER_BASE)

    loaded(EXPONENTS, exp_words)
    for half in range(2):
        for row in range(2):
            for tile in range(tiles):
                at = (half * 2 + row) * tiles + tile
                column = tile + (c if half == 0 else 1 - c) * tiles
                if half == 0:
                    exps[0, pl.ds(at, 1), :] = jnp.full((1, BLOCK), exp_words[0, row, column], jnp.int32)
                exps[1, pl.ds(at, 1), :] = jnp.full((1, BLOCK), exp_words[1, row, column], jnp.int32)
    encode_exps = exps[0, 0:2 * tiles, :]
    enc_mul[0:2 * tiles, :] = power_of_two(-encode_exps)
    later_tables = []

    def return_tables():
        if not later_tables:
            later_tables.append(True)
            return_exps = exps[1, 0:4 * tiles, :]
            enc_scale[0:2 * tiles, :] = power_of_two(exps[0, 0:2 * tiles, :]) * (1.0 / (2 * NX * NZ))
            ret_mul[0:4 * tiles, :] = power_of_two(-return_exps)
            ret_scale[0:4 * tiles, :] = power_of_two(return_exps)

    ready = set()

    def need(*blocks):
        for which in blocks:
            if which not in ready:
                ready.add(which)
                rows, first, count = piece(which)
                lanes = pl.ds(first, count)
                arrived(IN_SWAP + which, mine.at[:, rows, lanes])

    def encoded_pair(which, tile):
        block = order[which]
        rows = rows_of(block)
        lanes = slice(tile * BLOCK, (tile + 1) * BLOCK)
        factor = enc_mul[pl.ds((block // 2) * tiles + tile, 1), :]
        start = mine[0, rows, lanes].astype(F32)
        total = None
        for source in (mine[1, rows, lanes], mine[2, rows, lanes]):
            code = jnp.clip((source.astype(F32) - start) * factor, -CODE_LIMIT, CODE_LIMIT)
            code = code.astype(BF16).astype(F32)
            total = code if total is None else total + code
        return total.reshape(NZ, ZROWS, BLOCK)

    def span(k):
        lo, hi = CHUNKS[k][:2]
        return range(lo, hi)

    def part(k):
        lo, hi = CHUNKS[k][:2]
        return pl.ds(lo, hi - lo)

    def mode(k):
        return CHUNKS[k][2]

    def event(k, what):
        return STARTS[k] + what

    def fill(which, k):
        for tile in span(k):
            shards[tile, order[which]] = encoded_pair(which, tile).astype(BF16)

    def encode(k):
        if mode(k) != ZFIRST:
            need(0, 1, 2)
            for which, d in ((0, 2), (1, 1), (2, 3)):
                fill(which, k)
                for e in (2, 1, 3):
                    at = (z + e) % NZ
                    remote(
                        shards.at[part(k), order[which], at], x_in.at[d - 1, part(k), at], x_devs[d - 1],
                        SHARDS, event(k, FIRST),
                    )
        else:
            need(WHOLE)
            for which in range(4):
                fill(which, k)
            for d in (2, 1, 3):
                for e in (2, 1, 3):
                    at = (x + e) % NX
                    remote(
                        shards.at[part(k), at, (z + d) % NZ], z_in.at[d - 1, part(k), at], z_devs[d - 1],
                        SHARDS, event(k, FIRST),
                    )

    def send_owned(k):
        for d in (2, 1, 3):
            if mode(k) != ZFIRST:
                remote(
                    shards.at[part(k), (x + d) % NX, z], x_in.at[d - 1, part(k), z], x_devs[d - 1],
                    SHARDS, event(k, SECOND),
                )
            else:
                remote(
                    shards.at[part(k), x, (z + d) % NZ], z_in.at[d - 1, part(k), x], z_devs[d - 1],
                    SHARDS, event(k, SECOND),
                )

    def pair(k):
        need(3)
        for tile in span(k):
            t_wide[tile] = encoded_pair(3, tile)

    def first_total(k, tile, at):
        if mode(k) != ZFIRST:
            total, parts = t_wide[tile, at], x_in
        else:
            total, parts = shards[tile, at, z].astype(F32), z_in
        for d in range(3):
            total = total + parts[d, tile, at].astype(F32)
        return total

    def sum_first(k):
        arrived(event(k, FIRST), (x_in if mode(k) != ZFIRST else z_in).at[:, part(k), pl.ds(0, 3)])
        for d in (2, 1, 3):
            at = ((z if mode(k) != ZFIRST else x) + d) % NZ
            for tile in span(k):
                t_narrow[tile, at] = first_total(k, tile, at).astype(BF16)
            landing, devices = (z_in, z_devs) if mode(k) != ZFIRST else (x_in, x_devs)
            remote(t_narrow.at[part(k), at], landing.at[d - 1, part(k), 0], devices[d - 1], SUMS, event(k, SECOND))

    started = set()

    def step(k):
        return_tables()
        if IN_MOMENT not in started:
            started.add(IN_MOMENT)
            arrived(IN_MOMENT, moment)
        second = x_in if mode(k) == ZFIRST else z_in
        mine_at = x if mode(k) == ZFIRST else z
        arrived(event(k, SECOND), shards.at[part(k), pl.ds(0, 2), pl.ds(0, 3)])
        for tile in span(k):
            lanes = slice(tile * BLOCK, (tile + 1) * BLOCK)
            at = pl.ds((x // 2) * tiles + tile, 1)
            summed = first_total(k, tile, mine_at)
            for d in range(3):
                summed = summed + second[d, tile, 0].astype(F32)
            outer_grad = summed * enc_scale[at, :]
            new_moment = MOMENTUM_RATE * moment[:, lanes] + outer_grad
            moment_out[:, lanes] = new_moment
            outer_step = OUTER_RATE * (outer_grad + MOMENTUM_RATE * new_moment)
            code = jnp.clip(outer_step * ret_mul[at, :], -CODE_LIMIT, CODE_LIMIT)
            codes[tile, x, z] = code.astype(BF16)
        piece = codes.at[part(k), x, z]
        for d in (2, 1, 3):
            if mode(k) != ZFIRST:
                remote(piece, piece, z_devs[d - 1], CODES, event(k, CODES_IN + z))
            else:
                remote(piece, piece, x_devs[d - 1], CODES, event(k, CODES_IN + x))
        gather(k, piece, z if mode(k) != ZFIRST else x)

    def gather(k, piece, at):
        for d in (2, 1, 3):
            if mode(k) != ZFIRST:
                remote(piece, piece, x_devs[d - 1], GATHER, event(k, FAR_IN if d == 2 else NEAR_IN))
            else:
                remote(piece, piece, z_devs[d - 1], GATHER, event(k, FAR_IN))
            if mode(k) == BOTH:
                remote(piece, sib_codes.at[part(k), x, at], cross_devs[d - 1], TWICE, event(k, CORE_FAR))

    def to_sibling(k, block, arrival):
        remote(codes.at[part(k), block], sib_codes.at[part(k), block], sibling, TWICE if mode(k) == BOTH else CORE, event(k, arrival))

    line_order = [jnp.where(z < 2, at, 3 - at) for at in (1 - jnp.minimum(z, 3 - z), 2, 3)]

    def ring(k):
        for at in line_order if mode(k) != ZFIRST else (right, left, far):
            piece = codes.at[part(k), x, at] if mode(k) != ZFIRST else codes.at[part(k), at, z]
            arrived(event(k, CODES_IN + at), piece)
            gather(k, piece, at)
        if mode(k) != ZFIRST:
            to_sibling(k, x, CORE_NEAR)

    def land_near(k):
        arrived(event(k, NEAR_IN), codes.at[part(k), pl.ds(0, 2)])
        if mode(k) != BOTH:
            to_sibling(k, right, CORE_NEAR)
            to_sibling(k, left, CORE_NEAR)

    def land(k):
        if mode(k) == ZFIRST:
            arrived(event(k, FAR_IN), codes.at[part(k), pl.ds(0, 3)])
            remote(codes.at[part(k)], sib_codes.at[part(k)], sibling, CORE, event(k, CORE_FAR))
        else:
            arrived(event(k, FAR_IN), codes.at[part(k), 0])
            if mode(k) != BOTH:
                to_sibling(k, far, CORE_FAR)

    def apply(k, block, own):
        rows = rows_of(block)
        if not own and OTHER_BASE not in started:
            started.add(OTHER_BASE)
            loaded(OTHER_BASE, oth_base)
        for tile in span(k):
            lanes = slice(tile * BLOCK, (tile + 1) * BLOCK)
            at = pl.ds(((0 if own else 2) + block // 2) * tiles + tile, 1)
            code = (codes if own else sib_codes)[tile, block].reshape(XROWS, BLOCK).astype(F32)
            start = mine[0, rows, lanes] if own else oth_base[rows, lanes]
            out_lanes = pl.ds(pl.multiple_of((c if own else 1 - c) * width + tile * BLOCK, BLOCK), BLOCK)
            new_params[rows, out_lanes] = (start.astype(F32) + code * ret_scale[at, :]).astype(BF16)

    def own(k):
        apply(k, x, True)

    def own_near(k):
        apply(k, right, True)
        apply(k, left, True)

    def own_far(k):
        for block in order if mode(k) == ZFIRST else (far,):
            apply(k, block, True)

    def other_near(k):
        blocks = (x,) if mode(k) == BOTH else (x, right, left)
        arrived(event(k, CORE_NEAR), codes.at[part(k), pl.ds(0, len(blocks))])
        for block in blocks:
            apply(k, block, False)

    def other_far(k):
        blocks = {ONE: (far,), ZFIRST: order, BOTH: (far, right, left)}[mode(k)]
        arrived(event(k, CORE_FAR), codes.at[part(k), pl.ds(0, len(blocks))])
        for block in blocks:
            apply(k, block, False)

    stages = {
        ENCODE: encode, SEND_OWNED: send_owned, PAIR: pair, SUM: sum_first, STEP: step, RING: ring,
        LAND_NEAR: land_near, LAND: land, OWN: own, OWN_NEAR: own_near, OWN_FAR: own_far,
        OTHER_NEAR: other_near, OTHER_FAR: other_far,
    }
    steps_left = len(CHUNKS)
    for stage, k in SCHEDULE:
        stages[stage](k)
        if stage == STEP:
            steps_left -= 1
            if steps_left == 0:
                back = moment_out.at[other_rows]
                remote(back, new_momentum.at[:, own_cols], sibling, MOMENT, IN_MOMENT_BACK)
                new_momentum[:, own_cols] = moment_out[moment_rows]
    arrived(IN_MOMENT_BACK, new_momentum.at[:, oth_cols])

    sent(SWAP, mine.at[2])
    sent(SHARDS, shards.at[:, pl.ds(0, 3)])
    sent(SUMS, t_narrow.at[:, pl.ds(0, 3)])
    sent(CODES, t_narrow.at[:, pl.ds(0, 3)])
    sent(GATHER, codes.at[:, pl.ds(0, 3)])
    twice = sum(hi - lo for lo, hi, how in CHUNKS if how == BOTH)
    sent(CORE, codes.at[pl.ds(0, tiles - twice)])
    if twice:
        sent(TWICE, codes.at[pl.ds(0, twice)])
    sent(MOMENT, moment)


def store(params, momentum, params_out, momentum_out, sem):
    copies = [
        pltpu.make_async_copy(params, params_out, sem.at[0]), pltpu.make_async_copy(momentum, momentum_out, sem.at[1])
    ]
    for copy in copies:
        copy.start()
    for copy in copies:
        copy.wait()


def on_device(local_params, base_params, momentum, encode_exponents, return_exponents):
    _, rows, columns = local_params.shape
    width = columns // 2
    tiles = width // BLOCK
    table = pltpu.VMEM((-(-4 * tiles // 8) * 8, BLOCK), F32)
    hbm = pl.BlockSpec(memory_space=pltpu.HBM)
    vmem = pl.BlockSpec(memory_space=pltpu.VMEM)
    held = pl.pallas_call(
        kernel,
        name="outer_step",
        out_shape=(pltpu.VMEM((rows, columns), BF16), pltpu.VMEM(momentum.shape, F32)),
        in_specs=[hbm] * 5,
        out_specs=(vmem, vmem),
        scratch_shapes=[
            pltpu.SMEM((2,) + encode_exponents.shape, jnp.int32),
            pltpu.VMEM((3, rows, width), BF16),
            pltpu.VMEM((rows, width), BF16),
            pltpu.VMEM((2, -(-4 * tiles // 8) * 8, BLOCK), jnp.int32),
            table, table, table, table,
            pltpu.VMEM((tiles, NX, NZ, ZROWS, BLOCK), BF16),
            pltpu.VMEM((3, tiles, NZ, ZROWS, BLOCK), BF16),
            pltpu.VMEM((3, tiles, NX, ZROWS, BLOCK), BF16),
            pltpu.VMEM((tiles, NZ, ZROWS, BLOCK), F32),
            pltpu.VMEM((tiles, NZ, ZROWS, BLOCK), BF16),
            pltpu.VMEM((ZROWS, width), F32),
            pltpu.VMEM((ZROWS, width), F32),
            pltpu.VMEM((tiles, NX, NZ, ZROWS, BLOCK), BF16),
            pltpu.VMEM((tiles, NX, NZ, ZROWS, BLOCK), BF16),
            pltpu.SemaphoreType.DMA((LOADS,)),
            pltpu.SemaphoreType.DMA((SENDS,)),
            pltpu.SemaphoreType.DMA((ARRIVALS,)),
        ],
        compiler_params=pltpu.CompilerParams(
            collective_id=0, has_side_effects=True, vmem_limit_bytes=32 * 2**20
        ),
        cost_estimate=pl.CostEstimate(flops=20_000_000, bytes_accessed=4_500_000, transcendentals=0),
    )(*[
        pltpu.with_memory_space_constraint(array, pltpu.HBM)
        for array in (local_params, base_params, momentum, encode_exponents, return_exponents)
    ])
    return pl.pallas_call(
        store,
        name="store",
        out_shape=tuple(pltpu.HBM(array.shape, array.dtype) for array in held),
        in_specs=[vmem, vmem],
        out_specs=(hbm, hbm),
        scratch_shapes=[pltpu.SemaphoreType.DMA((2,))],
    )(*[pltpu.with_memory_space_constraint(array, pltpu.VMEM) for array in held])


def solution(mesh):
    return jax.shard_map(
        on_device,
        mesh=mesh,
        in_specs=(
            P("rep", None, "fsdp"),
            P(None, "fsdp"),
            P("rep", "fsdp"),
            P(None, "fsdp"),
            P(None, "fsdp"),
        ),
        out_specs=(P(None, "fsdp"), P("rep", "fsdp")),
        check_vma=False,
    )
```

```python
import jax
import jax.numpy as jnp
from jax import lax
from jax.experimental import pallas as pl
from jax.experimental.pallas import tpu as pltpu
from jax.sharding import PartitionSpec as P

BLOCK = 128
CODE_LIMIT = 448.0
MOMENTUM_RATE = 0.9
OUTER_RATE = 0.7
MESH = pl.DeviceIdType.MESH
BF16, F32 = jnp.bfloat16, jnp.float32
NX, NZ = 4, 4
ZROWS = 16
XROWS = NZ * ZROWS

ONE, ZFIRST, BOTH = range(3)
CHUNKS = ((0, 3, ONE), (3, 6, ONE), (6, 8, BOTH), (8, 9, ZFIRST), (9, 11, ZFIRST))
EXPONENTS, OTHER_BASE = range(2)
LOADS = 2
SWAP, SHARDS, SUMS, CODES, GATHER, CORE, MOMENT, TWICE = range(8)
SENDS = 8
IN_SWAP, IN_MOMENT, IN_MOMENT_BACK, IN_CHUNKS = 0, 5, 6, 7
Z_TILE = min([lo for lo, _, how in CHUNKS if how == ZFIRST], default=0)
WHOLE = 4
FIRST, SECOND, FAR_IN, CORE_FAR, CODES_IN, NEAR_IN, CORE_NEAR = 0, 1, 2, 3, 4, 8, 9


def chunk_starts():
    starts = [IN_CHUNKS]
    for _, _, how in CHUNKS:
        starts.append(starts[-1] + (8 if how == ZFIRST else 10))
    return starts


STARTS = chunk_starts()
ARRIVALS = STARTS[-1]
(
    ENCODE, SEND_OWNED, PAIR, SUM, STEP, RING, LAND_NEAR, LAND, OWN, OWN_NEAR, OWN_FAR, OTHER_NEAR, OTHER_FAR,
) = range(13)
SCHEDULE = (
    (ENCODE, 0), (ENCODE, 1), (ENCODE, 2), (PAIR, 0), (PAIR, 1), (PAIR, 2),
    (ENCODE, 3), (ENCODE, 4), (SEND_OWNED, 0), (SEND_OWNED, 1), (SEND_OWNED, 2), (SEND_OWNED, 3),
    (SEND_OWNED, 4), (SUM, 0), (SUM, 3), (SUM, 1), (SUM, 2), (SUM, 4),
    (STEP, 3), (STEP, 0), (STEP, 1), (STEP, 4), (STEP, 2), (RING, 3),
    (RING, 0), (OWN, 0), (RING, 4), (RING, 1), (OWN, 1), (RING, 2),
    (OWN, 2), (LAND, 3), (OWN_FAR, 3), (OTHER_NEAR, 2), (LAND_NEAR, 0), (LAND, 0),
    (OWN_NEAR, 0), (OWN_FAR, 0), (OTHER_FAR, 3), (OTHER_NEAR, 0), (OTHER_FAR, 0), (LAND_NEAR, 1),
    (LAND, 1), (OWN_NEAR, 1), (OWN_FAR, 1), (LAND, 4), (OWN_FAR, 4), (OTHER_NEAR, 1),
    (OTHER_FAR, 1), (LAND, 2), (OTHER_FAR, 2), (OWN_FAR, 2), (LAND_NEAR, 2), (OWN_NEAR, 2),
    (OTHER_FAR, 4),
)


def power_of_two(exponent):
    size = jnp.abs(exponent)
    result = jnp.ones(exponent.shape, F32)
    for bit in range(7):
        up, down = 2.0 ** (1 << bit), 2.0 ** -(1 << bit)
        factor = jnp.where(exponent < 0, down, up)
        result = result * jnp.where((size & (1 << bit)) != 0, factor, 1.0)
    return result


def kernel(
    params, base, momentum, enc_exp, ret_exp, new_params, new_momentum,
    exp_words, mine, oth_base, exps, enc_mul, enc_scale, ret_mul, ret_scale,
    shards, x_in, z_in, t_wide, t_narrow, moment, moment_out, codes, sib_codes,
    load_sem, send_sem, recv_sem,
):
    rep = lax.axis_index("rep")
    x, z, c = rep // (NZ * 2), (rep // 2) % NZ, rep % 2
    width = mine.shape[2]
    tiles = width // BLOCK

    def place(px, pz, pc):
        return {"rep": (px * NZ + pz) * 2 + pc}

    sibling = place(x, z, 1 - c)
    right, far, left = (x + 1) % NX, (x + 2) % NX, (x + 3) % NX
    x_devs = [place((x + d) % NX, z, c) for d in (1, 2, 3)]
    z_devs = [place(x, (z + d) % NZ, c) for d in (1, 2, 3)]
    cross_devs = [place((x + d) % NX, z, 1 - c) for d in (1, 2, 3)]

    def rows_of(block):
        return pl.ds(pl.multiple_of(block * XROWS, XROWS), XROWS)

    own_cols = pl.ds(pl.multiple_of(c * width, BLOCK), width)
    oth_cols = pl.ds(pl.multiple_of((1 - c) * width, BLOCK), width)

    def local(src, dst, sem):
        pltpu.make_async_copy(src, dst, load_sem.at[sem]).start()

    def beside_swap(src, dst, arrival):
        pltpu.make_async_copy(src, dst, recv_sem.at[arrival]).start()

    def remote(src, dst, device, send, arrival):
        pltpu.make_async_remote_copy(
            src_ref=src, dst_ref=dst, send_sem=send_sem.at[send], recv_sem=recv_sem.at[arrival],
            device_id=device, device_id_type=MESH,
        ).start()

    def take(sem, ref):
        pltpu.make_async_copy(ref, ref, sem).wait()

    def loaded(sem, ref):
        take(load_sem.at[sem], ref)

    def arrived(sem, ref):
        take(recv_sem.at[sem], ref)

    def sent(sem, ref):
        take(send_sem.at[sem], ref)

    barrier = pltpu.get_barrier_semaphore()
    for device in x_devs + z_devs + cross_devs + [sibling]:
        pl.semaphore_signal(barrier, inc=1, device_id=device, device_id_type=MESH)

    order = (far, right, left, x)
    first_z = Z_TILE * BLOCK

    def piece(which):
        if which == WHOLE:
            return pl.ds(0, NX * XROWS), first_z, width - first_z
        return rows_of(order[which]), 0, first_z

    def columns(core, first, count):
        return pl.ds(pl.multiple_of(core * width + first, BLOCK), count)

    pieces = (0, 1, 2, 3, WHOLE)
    pl.semaphore_wait(barrier, 10)

    for which in pieces:
        rows, first, count = piece(which)
        remote(
            params.at[0, rows, columns(1 - c, first, count)], mine.at[2, rows, pl.ds(first, count)],
            sibling, SWAP, IN_SWAP + which,
        )
    for which in pieces:
        rows, first, count = piece(which)
        lanes = pl.ds(first, count)
        beside_swap(base.at[rows, columns(c, first, count)], mine.at[0, rows, lanes], IN_SWAP + which)
        beside_swap(params.at[0, rows, columns(c, first, count)], mine.at[1, rows, lanes], IN_SWAP + which)
    local(enc_exp, exp_words.at[0], EXPONENTS)
    local(ret_exp, exp_words.at[1], EXPONENTS)

    moment_rows = pl.ds(pl.multiple_of(c * 8, 8), 8)
    other_rows = pl.ds(pl.multiple_of((1 - c) * 8, 8), 8)
    remote(momentum.at[:, oth_cols], moment.at[moment_rows], sibling, MOMENT, IN_MOMENT)
    beside_swap(momentum.at[:, own_cols], moment.at[moment_rows], IN_MOMENT)
    local(base.at[:, oth_cols], oth_base, OTHER_BASE)

    loaded(EXPONENTS, exp_words)
    for half in range(2):
        for row in range(2):
            for tile in range(tiles):
                at = (half * 2 + row) * tiles + tile
                column = tile + (c if half == 0 else 1 - c) * tiles
                if half == 0:
                    exps[0, pl.ds(at, 1), :] = jnp.full((1, BLOCK), exp_words[0, row, column], jnp.int32)
                exps[1, pl.ds(at, 1), :] = jnp.full((1, BLOCK), exp_words[1, row, column], jnp.int32)
    encode_exps = exps[0, 0:2 * tiles, :]
    enc_mul[0:2 * tiles, :] = power_of_two(-encode_exps)
    later_tables = []

    def return_tables():
        if not later_tables:
            later_tables.append(True)
            return_exps = exps[1, 0:4 * tiles, :]
            enc_scale[0:2 * tiles, :] = power_of_two(exps[0, 0:2 * tiles, :]) * (1.0 / (2 * NX * NZ))
            ret_mul[0:4 * tiles, :] = power_of_two(-return_exps)
            ret_scale[0:4 * tiles, :] = power_of_two(return_exps)

    ready = set()

    def need(*blocks):
        for which in blocks:
            if which not in ready:
                ready.add(which)
                rows, first, count = piece(which)
                lanes = pl.ds(first, count)
                arrived(IN_SWAP + which, mine.at[:, rows, lanes])

    def encoded_pair(which, tile):
        block = order[which]
        rows = rows_of(block)
        lanes = slice(tile * BLOCK, (tile + 1) * BLOCK)
        factor = enc_mul[pl.ds((block // 2) * tiles + tile, 1), :]
        start = mine[0, rows, lanes].astype(F32)
        total = None
        for source in (mine[1, rows, lanes], mine[2, rows, lanes]):
            code = jnp.clip((source.astype(F32) - start) * factor, -CODE_LIMIT, CODE_LIMIT)
            code = code.astype(BF16).astype(F32)
            total = code if total is None else total + code
        return total.reshape(NZ, ZROWS, BLOCK)

    def span(k):
        lo, hi = CHUNKS[k][:2]
        return range(lo, hi)

    def part(k):
        lo, hi = CHUNKS[k][:2]
        return pl.ds(lo, hi - lo)

    def mode(k):
        return CHUNKS[k][2]

    def event(k, what):
        return STARTS[k] + what

    def fill(which, k):
        for tile in span(k):
            shards[tile, order[which]] = encoded_pair(which, tile).astype(BF16)

    def encode(k):
        if mode(k) != ZFIRST:
            need(0, 1, 2)
            for which, d in ((0, 2), (1, 1), (2, 3)):
                fill(which, k)
                for e in (2, 1, 3):
                    at = (z + e) % NZ
                    remote(
                        shards.at[part(k), order[which], at], x_in.at[d - 1, part(k), at], x_devs[d - 1],
                        SHARDS, event(k, FIRST),
                    )
        else:
            need(WHOLE)
            for which in range(4):
                fill(which, k)
            for d in (2, 1, 3):
                for e in (2, 1, 3):
                    at = (x + e) % NX
                    remote(
                        shards.at[part(k), at, (z + d) % NZ], z_in.at[d - 1, part(k), at], z_devs[d - 1],
                        SHARDS, event(k, FIRST),
                    )

    def send_owned(k):
        for d in (2, 1, 3):
            if mode(k) != ZFIRST:
                remote(
                    shards.at[part(k), (x + d) % NX, z], x_in.at[d - 1, part(k), z], x_devs[d - 1],
                    SHARDS, event(k, SECOND),
                )
            else:
                remote(
                    shards.at[part(k), x, (z + d) % NZ], z_in.at[d - 1, part(k), x], z_devs[d - 1],
                    SHARDS, event(k, SECOND),
                )

    def pair(k):
        need(3)
        for tile in span(k):
            t_wide[tile] = encoded_pair(3, tile)

    def first_total(k, tile, at):
        if mode(k) != ZFIRST:
            total, parts = t_wide[tile, at], x_in
        else:
            total, parts = shards[tile, at, z].astype(F32), z_in
        for d in range(3):
            total = total + parts[d, tile, at].astype(F32)
        return total

    def sum_first(k):
        arrived(event(k, FIRST), (x_in if mode(k) != ZFIRST else z_in).at[:, part(k), pl.ds(0, 3)])
        for d in (2, 1, 3):
            at = ((z if mode(k) != ZFIRST else x) + d) % NZ
            for tile in span(k):
                t_narrow[tile, at] = first_total(k, tile, at).astype(BF16)
            landing, devices = (z_in, z_devs) if mode(k) != ZFIRST else (x_in, x_devs)
            remote(t_narrow.at[part(k), at], landing.at[d - 1, part(k), 0], devices[d - 1], SUMS, event(k, SECOND))

    started = set()

    def step(k):
        return_tables()
        if IN_MOMENT not in started:
            started.add(IN_MOMENT)
            arrived(IN_MOMENT, moment)
        second = x_in if mode(k) == ZFIRST else z_in
        mine_at = x if mode(k) == ZFIRST else z
        arrived(event(k, SECOND), shards.at[part(k), pl.ds(0, 2), pl.ds(0, 3)])
        for tile in span(k):
            lanes = slice(tile * BLOCK, (tile + 1) * BLOCK)
            at = pl.ds((x // 2) * tiles + tile, 1)
            summed = first_total(k, tile, mine_at)
            for d in range(3):
                summed = summed + second[d, tile, 0].astype(F32)
            outer_grad = summed * enc_scale[at, :]
            new_moment = MOMENTUM_RATE * moment[:, lanes] + outer_grad
            moment_out[:, lanes] = new_moment
            outer_step = OUTER_RATE * (outer_grad + MOMENTUM_RATE * new_moment)
            code = jnp.clip(outer_step * ret_mul[at, :], -CODE_LIMIT, CODE_LIMIT)
            codes[tile, x, z] = code.astype(BF16)
        piece = codes.at[part(k), x, z]
        for d in (2, 1, 3):
            if mode(k) != ZFIRST:
                remote(piece, piece, z_devs[d - 1], CODES, event(k, CODES_IN + z))
            else:
                remote(piece, piece, x_devs[d - 1], CODES, event(k, CODES_IN + x))
        gather(k, piece, z if mode(k) != ZFIRST else x)

    def gather(k, piece, at):
        for d in (2, 1, 3):
            if mode(k) != ZFIRST:
                remote(piece, piece, x_devs[d - 1], GATHER, event(k, FAR_IN if d == 2 else NEAR_IN))
            else:
                remote(piece, piece, z_devs[d - 1], GATHER, event(k, FAR_IN))
            if mode(k) == BOTH:
                remote(piece, sib_codes.at[part(k), x, at], cross_devs[d - 1], TWICE, event(k, CORE_FAR))

    def to_sibling(k, block, arrival):
        remote(codes.at[part(k), block], sib_codes.at[part(k), block], sibling, TWICE if mode(k) == BOTH else CORE, event(k, arrival))

    line_order = [jnp.where(z < 2, at, 3 - at) for at in (1 - jnp.minimum(z, 3 - z), 2, 3)]

    def ring(k):
        for at in line_order if mode(k) != ZFIRST else (right, left, far):
            piece = codes.at[part(k), x, at] if mode(k) != ZFIRST else codes.at[part(k), at, z]
            arrived(event(k, CODES_IN + at), piece)
            gather(k, piece, at)
        if mode(k) != ZFIRST:
            to_sibling(k, x, CORE_NEAR)

    def land_near(k):
        arrived(event(k, NEAR_IN), codes.at[part(k), pl.ds(0, 2)])
        if mode(k) != BOTH:
            to_sibling(k, right, CORE_NEAR)
            to_sibling(k, left, CORE_NEAR)

    def land(k):
        if mode(k) == ZFIRST:
            arrived(event(k, FAR_IN), codes.at[part(k), pl.ds(0, 3)])
            remote(codes.at[part(k)], sib_codes.at[part(k)], sibling, CORE, event(k, CORE_FAR))
        else:
            arrived(event(k, FAR_IN), codes.at[part(k), 0])
            if mode(k) != BOTH:
                to_sibling(k, far, CORE_FAR)

    def apply(k, block, own):
        rows = rows_of(block)
        if not own and OTHER_BASE not in started:
            started.add(OTHER_BASE)
            loaded(OTHER_BASE, oth_base)
        for tile in span(k):
            lanes = slice(tile * BLOCK, (tile + 1) * BLOCK)
            at = pl.ds(((0 if own else 2) + block // 2) * tiles + tile, 1)
            code = (codes if own else sib_codes)[tile, block].reshape(XROWS, BLOCK).astype(F32)
            start = mine[0, rows, lanes] if own else oth_base[rows, lanes]
            out_lanes = pl.ds(pl.multiple_of((c if own else 1 - c) * width + tile * BLOCK, BLOCK), BLOCK)
            new_params[rows, out_lanes] = (start.astype(F32) + code * ret_scale[at, :]).astype(BF16)

    def own(k):
        apply(k, x, True)

    def own_near(k):
        apply(k, right, True)
        apply(k, left, True)

    def own_far(k):
        for block in order if mode(k) == ZFIRST else (far,):
            apply(k, block, True)

    def other_near(k):
        blocks = (x,) if mode(k) == BOTH else (x, right, left)
        arrived(event(k, CORE_NEAR), codes.at[part(k), pl.ds(0, len(blocks))])
        for block in blocks:
            apply(k, block, False)

    def other_far(k):
        blocks = {ONE: (far,), ZFIRST: order, BOTH: (far, right, left)}[mode(k)]
        arrived(event(k, CORE_FAR), codes.at[part(k), pl.ds(0, len(blocks))])
        for block in blocks:
            apply(k, block, False)

    stages = {
        ENCODE: encode, SEND_OWNED: send_owned, PAIR: pair, SUM: sum_first, STEP: step, RING: ring,
        LAND_NEAR: land_near, LAND: land, OWN: own, OWN_NEAR: own_near, OWN_FAR: own_far,
        OTHER_NEAR: other_near, OTHER_FAR: other_far,
    }
    steps_left = len(CHUNKS)
    for stage, k in SCHEDULE:
        stages[stage](k)
        if stage == STEP:
            steps_left -= 1
            if steps_left == 0:
                back = moment_out.at[other_rows]
                remote(back, new_momentum.at[:, own_cols], sibling, MOMENT, IN_MOMENT_BACK)
                new_momentum[:, own_cols] = moment_out[moment_rows]
    arrived(IN_MOMENT_BACK, new_momentum.at[:, oth_cols])

    sent(SWAP, mine.at[2])
    sent(SHARDS, shards.at[:, pl.ds(0, 3)])
    sent(SUMS, t_narrow.at[:, pl.ds(0, 3)])
    sent(CODES, t_narrow.at[:, pl.ds(0, 3)])
    sent(GATHER, codes.at[:, pl.ds(0, 3)])
    twice = sum(hi - lo for lo, hi, how in CHUNKS if how == BOTH)
    sent(CORE, codes.at[pl.ds(0, tiles - twice)])
    if twice:
        sent(TWICE, codes.at[pl.ds(0, twice)])
    sent(MOMENT, moment)


def store(params, momentum, params_out, momentum_out, sem):
    copies = [
        pltpu.make_async_copy(params, params_out, sem.at[0]), pltpu.make_async_copy(momentum, momentum_out, sem.at[1])
    ]
    for copy in copies:
        copy.start()
    for copy in copies:
        copy.wait()


def on_device(local_params, base_params, momentum, encode_exponents, return_exponents):
    _, rows, columns = local_params.shape
    width = columns // 2
    tiles = width // BLOCK
    table = pltpu.VMEM((-(-4 * tiles // 8) * 8, BLOCK), F32)
    hbm = pl.BlockSpec(memory_space=pltpu.HBM)
    vmem = pl.BlockSpec(memory_space=pltpu.VMEM)
    held = pl.pallas_call(
        kernel,
        name="outer_step",
        out_shape=(pltpu.VMEM((rows, columns), BF16), pltpu.VMEM(momentum.shape, F32)),
        in_specs=[hbm] * 5,
        out_specs=(vmem, vmem),
        scratch_shapes=[
            pltpu.SMEM((2,) + encode_exponents.shape, jnp.int32),
            pltpu.VMEM((3, rows, width), BF16),
            pltpu.VMEM((rows, width), BF16),
            pltpu.VMEM((2, -(-4 * tiles // 8) * 8, BLOCK), jnp.int32),
            table, table, table, table,
            pltpu.VMEM((tiles, NX, NZ, ZROWS, BLOCK), BF16),
            pltpu.VMEM((3, tiles, NZ, ZROWS, BLOCK), BF16),
            pltpu.VMEM((3, tiles, NX, ZROWS, BLOCK), BF16),
            pltpu.VMEM((tiles, NZ, ZROWS, BLOCK), F32),
            pltpu.VMEM((tiles, NZ, ZROWS, BLOCK), BF16),
            pltpu.VMEM((ZROWS, width), F32),
            pltpu.VMEM((ZROWS, width), F32),
            pltpu.VMEM((tiles, NX, NZ, ZROWS, BLOCK), BF16),
            pltpu.VMEM((tiles, NX, NZ, ZROWS, BLOCK), BF16),
            pltpu.SemaphoreType.DMA((LOADS,)),
            pltpu.SemaphoreType.DMA((SENDS,)),
            pltpu.SemaphoreType.DMA((ARRIVALS,)),
        ],
        compiler_params=pltpu.CompilerParams(
            collective_id=0, has_side_effects=True, vmem_limit_bytes=32 * 2**20
        ),
        cost_estimate=pl.CostEstimate(flops=20_000_000, bytes_accessed=4_500_000, transcendentals=0),
    )(*[
        pltpu.with_memory_space_constraint(array, pltpu.HBM)
        for array in (local_params, base_params, momentum, encode_exponents, return_exponents)
    ])
    return pl.pallas_call(
        store,
        name="store",
        out_shape=tuple(pltpu.HBM(array.shape, array.dtype) for array in held),
        in_specs=[vmem, vmem],
        out_specs=(hbm, hbm),
        scratch_shapes=[pltpu.SemaphoreType.DMA((2,))],
    )(*[pltpu.with_memory_space_constraint(array, pltpu.VMEM) for array in held])


def solution(mesh):
    return jax.shard_map(
        on_device,
        mesh=mesh,
        in_specs=(
            P("rep", None, "fsdp"),
            P(None, "fsdp"),
            P("rep", "fsdp"),
            P(None, "fsdp"),
            P(None, "fsdp"),
        ),
        out_specs=(P(None, "fsdp"), P("rep", "fsdp")),
        check_vma=False,
    )
```
